32 devices in a mesh: tm: 8 (over y, x, core), tensor: 4 (over z).
Axes of the slice: x: 2, y: 2, z: 4, core: 2. Of those that a mesh axis runs over, the one named last changes fastest.
Arguments:
- latents: float32 [8, 1024, 3072], P('tm', None, 'tensor'), may hold values from -104 to 104
- noise: bfloat16 [8, 1024, 3072], P('tm', None, 'tensor'), may hold values from -5 to 5
- qkv_weight: bfloat16 [3072, 3, 3072], P(None, None, 'tensor'), may hold values from -0.108253175 to 0.108253175
- qk_gains: float32 [2, 3072], P(None, 'tensor'), may hold values from 0.45 to 6.6
- out_weight: bfloat16 [3072, 3072], P('tensor'), may hold values from -0.109375 to 0.109375
- modulation: bfloat16 [64, 3, 3072], P(None, None, 'tensor'), may hold values from -3 to 3
- step_sizes: float32 [64], replicated, may hold values from 0.02 to 0.08
- window_start: int32 [1], replicated, may hold values from 0 to 56
Outputs:
- updated: float32 [8, 1024, 3072], P('tm', None, 'tensor')
- velocity_out: bfloat16 [8, 1024, 3072], P('tm', None, 'tensor')
- slot_errors: float32 [8], P('tm')
The draws below stay inside these ranges and needn't reach their ends.
All inputs are finite; a program needn't handle non-finite values.
Results may differ from the reference program's by a relative error of at most 0.012.
Values may be sent and summed in bfloat16 or wider, within the bound.
A program may use at most 192 MiB of HBM per device.

```python
import math
import jax
import jax.numpy as jnp
from jax import lax

D = 3072
HEADS = 24
HEAD = 128
SEQ = 1024
STEPS = 64
WINDOW = 8
N_TENSOR = 4


def feature_scale(key, width):
    rising = jnp.exp(math.log(3.0) * jnp.arange(width, dtype=jnp.float32) / width)
    return rising * jax.random.uniform(key, (width,), jnp.float32, 0.6, 1.6)


def draw_latents(key, part):
    key = jax.random.fold_in(key, 11)
    key_base, key_scale = jax.random.split(key, 2)
    scale = feature_scale(key_scale, D)
    base = jax.random.truncated_normal(key_base, -4.0, 4.0, (WINDOW, SEQ, D), jnp.float32)
    return base * scale


def draw_noise(key, part):
    key = jax.random.fold_in(key, 12)
    key_base, key_scale = jax.random.split(key, 2)
    scale = 0.15 * feature_scale(key_scale, D)
    base = jax.random.truncated_normal(key_base, -4.0, 4.0, (WINDOW, SEQ, D), jnp.float32)
    return (base * scale).astype(jnp.bfloat16)


def draw_qkv_weight(key, part):
    key = jax.random.fold_in(key, 13)
    key_query, key_key, key_value = jax.random.split(key, 3)
    factor = D ** (-0.5)
    w_query = factor * jax.random.truncated_normal(key_query, -4.0, 4.0, (D, D), jnp.float32)
    w_key = factor * jax.random.truncated_normal(key_key, -4.0, 4.0, (D, D), jnp.float32)
    w_value = factor * jax.random.truncated_normal(key_value, -4.0, 4.0, (D, D), jnp.float32)
    return jnp.stack([w_query, w_key, w_value], axis=1).astype(jnp.bfloat16)


def draw_qk_gains(key, part):
    key = jax.random.fold_in(key, 14)
    key_heads, key_jitter = jax.random.split(key, 2)
    upper = math.log(2.0)
    strength = jnp.exp(jax.random.uniform(key_heads, (1, HEADS, 1), jnp.float32, math.log(0.5), upper))
    jitter = jax.random.uniform(key_jitter, (2, HEADS, HEAD), jnp.float32, 0.9, 1.1)
    return (strength * jitter).reshape(2, D)


def level_of(rng, extent, pieces, smallest, largest):
    def one(position, blocks):
        heights = jax.random.uniform(jax.random.fold_in(jax.random.fold_in(rng, 6), position), (blocks,), jnp.float32, smallest / len(pieces), largest / len(pieces))
        return jnp.repeat(jnp.exp(heights), extent[position] // blocks).reshape((-1,) + (1,) * (len(extent) - position - 1))

    level = one(*pieces[0])
    for cut in pieces[1:]:
        level = level * one(*cut)
    return level


def scatter_about(stream_key, shape, deviation, reach, cuts=(), held_as=jnp.bfloat16):
    gain = level_of(stream_key, shape, cuts, -0.22, 0.18) if cuts else 1.0
    array = jax.random.normal(stream_key, shape, jnp.float32) * deviation * gain
    return jnp.minimum(jnp.maximum(array, -reach), reach).astype(held_as)


def setup_inputs(seed: int = 0) -> dict:
    arg_keys = jax.random.split(jax.random.key(seed), 9)
    return {
        "latents": draw_latents(jax.random.fold_in(arg_keys[8], 71), 0),
        "noise": draw_noise(jax.random.fold_in(arg_keys[8], 71), 0),
        "qkv_weight": draw_qkv_weight(jax.random.fold_in(arg_keys[8], 71), 0),
        "qk_gains": draw_qk_gains(jax.random.fold_in(arg_keys[8], 71), 0),
        "out_weight": scatter_about(arg_keys[4], (D, D), D ** -0.5, 0.109375, ((0, 4),)),
        "modulation": scatter_about(arg_keys[5], (STEPS, 3, D), 0.5, 3.0, ((2, 4),)),
        "step_sizes": jnp.clip(jnp.exp(jax.random.uniform(arg_keys[6], (STEPS,), jnp.float32, math.log(0.02), math.log(0.08))), 0.02, 0.08),
        "window_start": jax.random.randint(arg_keys[7], (1,), 0, STEPS - WINDOW + 1).astype(jnp.int32),
    }


epsilon = 1e-06

def rms_scale(vectors, gain_rows):
    power = lax.optimization_barrier(jnp.mean(vectors * vectors, axis=-1, keepdims=True))
    return vectors * lax.rsqrt(power + epsilon) * gain_rows

def reference(latents, noise, qkv_weight, qk_gains, out_weight, modulation, step_sizes, window_start):
    offset = window_start[0]
    window_mod = lax.dynamic_slice_in_dim(modulation, offset, WINDOW, 0).astype(jnp.float32)
    window_steps = lax.dynamic_slice_in_dim(step_sizes, offset, WINDOW, 0)
    gain_rows = qk_gains.reshape(2, HEADS, HEAD)
    scaling = 1.0 / math.sqrt(HEAD)
    group_in = D // N_TENSOR

    def velocity_of(inputs):
        state, mod_rows = inputs
        row_mean = lax.optimization_barrier(jnp.mean(state, axis=1, keepdims=True))
        row_var = lax.optimization_barrier(jnp.mean(state * state, axis=1, keepdims=True)) - row_mean * row_mean
        modulated = ((state - row_mean) * lax.rsqrt(row_var + epsilon) * (1.0 + mod_rows[1]) + mod_rows[0]).astype(jnp.bfloat16)
        projected = jnp.dot(modulated, qkv_weight.reshape(D, 3 * D), preferred_element_type=jnp.float32)
        projected = projected.reshape(SEQ, 3, HEADS, HEAD)
        queries = rms_scale(projected[:, 0], gain_rows[0]).astype(jnp.bfloat16)
        keys_normed = rms_scale(projected[:, 1], gain_rows[1]).astype(jnp.bfloat16)
        values_heads = projected[:, 2].astype(jnp.bfloat16)
        scores = jnp.einsum('qhd,khd->hqk', queries.astype(jnp.float32), keys_normed.astype(jnp.float32)) * scaling
        attn_weights = jax.nn.softmax(scores, axis=-1).astype(jnp.bfloat16)
        attended = jnp.einsum('hqk,khd->qhd', attn_weights.astype(jnp.float32), values_heads.astype(jnp.float32))
        attended = attended.astype(jnp.bfloat16).reshape(SEQ, D)

        def group_term(group):
            start = (group * group_in).astype(jnp.int32)
            cols = lax.dynamic_slice_in_dim(attended, start, group_in, 1)
            rows = lax.dynamic_slice_in_dim(out_weight, start, group_in, 0)
            return jnp.dot(cols, rows, preferred_element_type=jnp.float32).astype(jnp.bfloat16)
        head_partials = lax.map(group_term, jnp.arange(N_TENSOR, dtype=jnp.int32))
        branch = lax.optimization_barrier(jnp.sum(head_partials.astype(jnp.float32), axis=0))
        return state + mod_rows[2] * branch
    velocity = lax.map(velocity_of, (latents, window_mod))
    increment = -window_steps[:, None, None] * velocity + noise.astype(jnp.float32)
    running = jnp.cumsum(increment, axis=0)
    earlier = jnp.concatenate([jnp.zeros((1, SEQ, D), jnp.float32), running[:-1]], axis=0)
    updated = latents[0][None] + earlier
    change = updated - latents
    slot_errors = lax.optimization_barrier(jnp.mean(change * change, axis=(1, 2)))
    return (updated, velocity.astype(jnp.bfloat16), slot_errors)
```

```python
import functools
import math

import jax
import jax.numpy as jnp
from jax import lax
from jax.experimental import pallas as pl
from jax.experimental.pallas import tpu as pltpu
from jax.sharding import PartitionSpec as P

HEAD = 128
HDR = 16
CHUNK = 256
epsilon = 1e-06
f32 = jnp.float32
bf16 = jnp.bfloat16


def kernel(
    n, tm_size, chunk,
    x_ref, noise_hbm, w_hbm, gains_ref, wo_hbm, mod_ref, step_ref,
    upd_ref, vel_ref, err_ref,
    gat, wbuf, wo, qkv, rbuf, tsend, trecv, noise, modb, att, erracc, ebuf,
    load_sem, ag_send, ag_recv, rs_send, rs_recv, t_send, t_recv, e_send, e_recv,
):
    z = lax.axis_index("tensor")
    slot = lax.axis_index("tm")
    length, width = x_ref.shape
    full = n * width
    nc = length // chunk
    heads = width // HEAD
    levels = tm_size.bit_length() - 1
    first = slot == 0

    loads = [
        pltpu.make_async_copy(
            w_hbm.at[j], wbuf.at[pl.ds(j * full, full)], load_sem.at[j]
        )
        for j in range(3)
    ]
    loads.append(pltpu.make_async_copy(wo_hbm, wo, load_sem.at[3]))
    loads.append(pltpu.make_async_copy(noise_hbm, noise, load_sem.at[4]))

    def crows(c, base=0):
        return pl.ds(pl.multiple_of(base + c * chunk, 16), chunk)

    partners = []
    for k in range(levels):
        bit = lax.rem(slot // (1 << k), 2)
        partners.append((slot + (1 - 2 * bit) * (1 << k), bit))

    barrier = pltpu.get_barrier_semaphore()
    for d in range(1, n):
        pl.semaphore_signal(
            barrier, inc=1, device_id={"tensor": lax.rem(z + d, n)},
            device_id_type=pl.DeviceIdType.MESH,
        )
    for partner, _ in partners:
        pl.semaphore_signal(
            barrier, inc=1, device_id={"tm": partner},
            device_id_type=pl.DeviceIdType.MESH,
        )

    gat[z, pl.ds(0, HDR), :] = mod_ref[...].astype(bf16)

    def cast(c, carry):
        gat[z, crows(c, HDR), :] = x_ref[crows(c), :].astype(bf16)
        return carry

    lax.fori_loop(0, nc, cast, 0)
    pl.semaphore_wait(barrier, n - 1 + levels)

    right = jnp.minimum(z + 1, n - 1)
    left = jnp.maximum(z - 1, 0)

    def ag(s, c, way):
        rows = pl.ds(0, HDR) if c is None else crows(c, HDR)
        i = nc if c is None else c
        return pltpu.make_async_remote_copy(
            src_ref=gat.at[s, rows], dst_ref=gat.at[s, rows],
            send_sem=ag_send.at[way, s, i], recv_sem=ag_recv.at[s, i],
            device_id={"tensor": right if way == 0 else left},
            device_id_type=pl.DeviceIdType.MESH,
        )

    def own(c):
        @pl.when(z < n - 1)
        def _():
            ag(z, c, 0).start()

        @pl.when(z > 0)
        def _():
            ag(z, c, 1).start()

    def forward(d, c):
        @pl.when(z >= d)
        def _():
            ag(z - d, c, 0).wait_recv()

            @pl.when(z < n - 1)
            def _():
                ag(z - d, c, 0).start()

        @pl.when(z + d < n)
        def _():
            ag(z + d, c, 1).wait_recv()

            @pl.when(z > 0)
            def _():
                ag(z + d, c, 1).start()

    own(None)

    def own_loop(c, carry):
        own(c)
        return carry

    lax.fori_loop(0, nc, own_loop, 0)
    for load in loads:
        load.start()

    for d in range(1, n):
        forward(d, None)
        if d < n - 1:

            def forward_loop(c, carry, d=d):
                forward(d, c)
                return carry

            lax.fori_loop(0, nc, forward_loop, 0)

    for load in loads:
        load.wait()

    def project(c, carry):
        forward(n - 1, c)
        rows = crows(c, HDR)
        total = jnp.zeros((chunk, 1), f32)
        square = jnp.zeros((chunk, 1), f32)
        for s in range(n):
            part = gat[s, rows, :].astype(f32)
            total += jnp.sum(part, axis=1, keepdims=True)
            square += jnp.sum(part * part, axis=1, keepdims=True)
        mean = total * (1.0 / full)
        var = square * (1.0 / full) - mean * mean
        rstd = lax.rsqrt(var + epsilon)
        for s in range(n):
            head_rows = gat[s, pl.ds(0, HDR), :].astype(f32)
            part = gat[s, rows, :].astype(f32)
            modb[:, s * width : (s + 1) * width] = (
                (part - mean) * rstd * (1.0 + head_rows[1:2]) + head_rows[0:1]
            ).astype(bf16)
        for j in range(3):
            out = jnp.dot(
                modb[...], wbuf[j * full : (j + 1) * full, :], preferred_element_type=f32
            )
            if j == 2:
                qkv[j, crows(c), :] = out.astype(bf16)
            else:
                for h in range(heads):
                    cols = slice(h * HEAD, (h + 1) * HEAD)
                    vec = out[:, cols]
                    power = jnp.mean(vec * vec, axis=1, keepdims=True)
                    qkv[j, crows(c), cols] = (
                        vec * lax.rsqrt(power + epsilon) * gains_ref[j : j + 1, cols]
                    ).astype(bf16)
        return carry

    lax.fori_loop(0, nc, project, 0)

    def prow(t, c):
        return pl.ds(pl.multiple_of(t * length + c * chunk, 16), chunk)

    def rs(t, c, way):
        if way == 0:
            place = t
        else:
            place = jnp.where(t == z - 1, n, t)
        return pltpu.make_async_remote_copy(
            src_ref=wbuf.at[prow(t, c)], dst_ref=rbuf.at[place, crows(c)],
            send_sem=rs_send.at[way, t, c], recv_sem=rs_recv.at[way, t, c],
            device_id={"tensor": right if way == 0 else left},
            device_id_type=pl.DeviceIdType.MESH,
        )

    def tx(k, c):
        return pltpu.make_async_remote_copy(
            src_ref=tsend.at[k, crows(c)], dst_ref=trecv.at[k, crows(c)],
            send_sem=t_send.at[k, c], recv_sem=t_recv.at[k, c],
            device_id={"tm": partners[k][0]}, device_id_type=pl.DeviceIdType.MESH,
        )

    exponent = math.log2(math.e) / math.sqrt(HEAD)

    def stage_attend(c):
        def one_head(h, carry):
            cols = pl.ds(pl.multiple_of(h * HEAD, HEAD), HEAD)
            scores = lax.dot_general(
                qkv[0, crows(c), cols], qkv[1, :, cols], (((1,), (1,)), ((), ())),
                preferred_element_type=f32,
            )
            top = jnp.max(scores, axis=1, keepdims=True)
            weights = jnp.exp2((scores - top) * exponent)
            norm = jnp.sum(weights, axis=1, keepdims=True)
            out = jnp.dot(weights.astype(bf16), qkv[2, :, cols], preferred_element_type=f32)
            att[:, cols] = (out / norm).astype(bf16)
            return carry

        lax.fori_loop(0, heads, one_head, 0, unroll=3)

        def one_part(t, carry):
            cols = pl.ds(pl.multiple_of(t * width, 128), width)
            part = jnp.dot(att[...], wo[:, cols], preferred_element_type=f32)
            wbuf[prow(t, c), :] = part.astype(bf16)
            return carry

        lax.fori_loop(0, n, one_part, 0)

        @pl.when(z == 0)
        def _():
            for t in range(n - 1, 0, -1):
                rs(t, c, 0).start()

        @pl.when(z == n - 1)
        def _():
            for t in range(n - 1):
                rs(t, c, 1).start()

    def stage_join(c):
        for t in range(n - 1, 0, -1):
            @pl.when((z > 0) & (z < t))
            def _():
                rs(t, c, 0).wait_recv()
                wbuf[prow(t, c), :] = (
                    wbuf[prow(t, c), :].astype(f32) + rbuf[t, crows(c), :].astype(f32)
                ).astype(bf16)
                rs(t, c, 0).start()

            u = n - 1 - t

            @pl.when((z < n - 1) & (z > u))
            def _():
                rs(u, c, 1).wait_recv()
                wbuf[prow(u, c), :] = (
                    wbuf[prow(u, c), :].astype(f32) + rbuf[u, crows(c), :].astype(f32)
                ).astype(bf16)
                rs(u, c, 1).start()

    def stage_velocity(c):
        rows = crows(c)

        @pl.when(z > 0)
        def _():
            rs(z, c, 0).wait_recv()

        @pl.when(z < n - 1)
        def _():
            pltpu.make_async_remote_copy(
                src_ref=wbuf.at[prow(z, c)], dst_ref=rbuf.at[n, rows],
                send_sem=rs_send.at[1, z, c], recv_sem=rs_recv.at[1, z, c],
                device_id={"tensor": right}, device_id_type=pl.DeviceIdType.MESH,
            ).wait_recv()

        branch = wbuf[prow(z, c), :].astype(f32)
        upd_ref[rows, :] = branch

        @pl.when(z > 0)
        def _():
            upd_ref[rows, :] = upd_ref[rows, :] + rbuf[z, rows, :].astype(f32)

        @pl.when(z < n - 1)
        def _():
            upd_ref[rows, :] = upd_ref[rows, :] + rbuf[n, rows, :].astype(f32)

        state = x_ref[rows, :]
        velocity = state + mod_ref[2:3, :] * upd_ref[rows, :]
        vel_ref[rows, :] = velocity.astype(bf16)
        start = jnp.where(first, state, jnp.zeros_like(state))
        upd_ref[rows, :] = start
        tsend[0, rows, :] = (
            noise[rows, :].astype(f32) - step_ref[0] * velocity + start
        ).astype(bf16)
        tx(0, c).start()

    def stage_prefix(k, c):
        rows = crows(c)
        tx(k, c).wait_recv()
        arrived = trecv[k, rows, :].astype(f32)
        if k < levels - 1:
            tsend[k + 1, rows, :] = (tsend[k, rows, :].astype(f32) + arrived).astype(bf16)
            tx(k + 1, c).start()
        keep = partners[k][1].astype(f32)
        now = upd_ref[rows, :] + keep * arrived
        upd_ref[rows, :] = now
        if k == levels - 1:
            change = now - x_ref[rows, :]
            erracc[...] += jnp.sum(
                (change * change).reshape(chunk // 8, 8, width), axis=0
            )

    erracc[...] = jnp.zeros_like(erracc)
    lag = 2

    def turn(i, carry):
        @pl.when(i < nc)
        def _():
            stage_attend(i)

        @pl.when((i >= 1) & (i < nc + 1))
        def _():
            stage_join(i - 1)

        @pl.when((i >= lag) & (i < nc + lag))
        def _():
            stage_velocity(i - lag)

        for k in range(levels):
            @pl.when((i >= lag + 1 + k) & (i < nc + lag + 1 + k))
            def _(k=k):
                stage_prefix(k, i - (lag + 1 + k))

        return carry

    lax.fori_loop(0, nc + lag + levels, turn, 0)

    ebuf[z] = jnp.zeros((8, 128), f32) + jnp.sum(erracc[...])

    def ex(d):
        return pltpu.make_async_remote_copy(
            src_ref=ebuf.at[z], dst_ref=ebuf.at[z],
            send_sem=e_send.at[d], recv_sem=e_recv.at[d],
            device_id={"tensor": lax.rem(z + d, n)}, device_id_type=pl.DeviceIdType.MESH,
        )

    for d in range(1, n):
        ex(d).start()

    def drain(c, carry):
        for s in range(n):
            @pl.when((z < n - 1) & (s <= z))
            def _():
                ag(s, c, 0).wait_send()

            @pl.when((z > 0) & (s >= z))
            def _():
                ag(s, c, 1).wait_send()

            @pl.when(z < s)
            def _():
                rs(s, c, 0).wait_send()

            @pl.when(z > s)
            def _():
                rs(s, c, 1).wait_send()

        for k in range(levels):
            tx(k, c).wait_send()
        return carry

    lax.fori_loop(0, nc, drain, 0)
    for s in range(n):
        @pl.when((z < n - 1) & (s <= z))
        def _():
            ag(s, None, 0).wait_send()

        @pl.when((z > 0) & (s >= z))
        def _():
            ag(s, None, 1).wait_send()

    for d in range(1, n):
        ex(d).wait()
    total = ebuf[0]
    for s in range(1, n):
        total = total + ebuf[s]
    err_ref[...] = total


def body(latents, noise, qkv_weight, qk_gains, out_weight, modulation, step_sizes, window_start):
    n = lax.axis_size("tensor")
    tm_size = lax.axis_size("tm")
    offset = window_start[0] + lax.axis_index("tm")
    _, length, width = latents.shape
    full = n * width
    mod_rows = lax.dynamic_index_in_dim(
        modulation.transpose(1, 0, 2), offset, 1, keepdims=False
    ).astype(f32)
    mod_rows = jnp.pad(mod_rows, ((0, HDR - 3), (0, 0)))
    step_size = lax.dynamic_slice_in_dim(step_sizes, offset, 1, 0)
    chunk = CHUNK
    nc = length // chunk
    levels = tm_size.bit_length() - 1
    vmem = pl.BlockSpec(memory_space=pltpu.VMEM)
    hbm = pl.BlockSpec(memory_space=pl.ANY)
    dma = pltpu.SemaphoreType.DMA
    updated, velocity, err = pl.pallas_call(
        functools.partial(kernel, n, tm_size, chunk),
        out_shape=(
            jax.ShapeDtypeStruct((length, width), f32),
            jax.ShapeDtypeStruct((length, width), bf16),
            jax.ShapeDtypeStruct((8, 128), f32),
        ),
        in_specs=[vmem, hbm, hbm, vmem, hbm, vmem, pl.BlockSpec(memory_space=pltpu.SMEM)],
        out_specs=(vmem, vmem, vmem),
        scratch_shapes=[
            pltpu.VMEM((n, HDR + length, width), bf16),
            pltpu.VMEM((3 * full, width), bf16),
            pltpu.VMEM((width, full), bf16),
            pltpu.VMEM((3, length, width), bf16),
            pltpu.VMEM((n + 1, length, width), bf16),
            pltpu.VMEM((levels, length, width), bf16),
            pltpu.VMEM((levels, length, width), bf16),
            pltpu.VMEM((length, width), bf16),
            pltpu.VMEM((chunk, full), bf16),
            pltpu.VMEM((chunk, width), bf16),
            pltpu.VMEM((8, width), f32),
            pltpu.VMEM((n, 8, 128), f32),
            dma((5,)),
            dma((2, n, nc + 1)),
            dma((n, nc + 1)),
            dma((2, n, nc)),
            dma((2, n, nc)),
            dma((levels, nc)),
            dma((levels, nc)),
            dma((n,)),
            dma((n,)),
        ],
        compiler_params=pltpu.CompilerParams(
            collective_id=0, has_side_effects=True, vmem_limit_bytes=62 * 2**20
        ),
    )(
        latents[0], noise[0], qkv_weight.transpose(1, 0, 2), qk_gains, out_weight,
        mod_rows, step_size,
    )
    return (updated[None], velocity[None], err[0, :1] / (length * full))


def solution(mesh):
    return jax.shard_map(
        body,
        mesh=mesh,
        in_specs=(
            P("tm", None, "tensor"),
            P("tm", None, "tensor"),
            P(None, None, "tensor"),
            P(None, "tensor"),
            P("tensor", None),
            P(None, None, "tensor"),
            P(),
            P(),
        ),
        out_specs=(P("tm", None, "tensor"), P("tm", None, "tensor"), P("tm")),
        check_vma=False,
    )
```

```python
import functools
import math

import jax
import jax.numpy as jnp
from jax import lax
from jax.experimental import pallas as pl
from jax.experimental.pallas import tpu as pltpu
from jax.sharding import PartitionSpec as P

HEAD = 128
HDR = 16
CHUNK = 256
SPLIT = 2
epsilon = 1e-06
f32 = jnp.float32
bf16 = jnp.bfloat16


def kernel(
    n, tm_size, chunk,
    x_ref, noise_hbm, w_hbm, gains_ref, wo_hbm, mod_ref, step_ref,
    upd_ref, vel_ref, err_ref,
    gat, wbuf, wo, qkv, rbuf, tsend, trecv, noise, modb, att, erracc, ebuf,
    load_sem, ag_send, ag_recv, rs_send, rs_recv, t_send, t_recv, e_send, e_recv, gate,
):
    z = lax.axis_index("tensor")
    slot = lax.axis_index("tm")
    length, width = x_ref.shape
    full = n * width
    nc = length // chunk
    sub = chunk // SPLIT
    ns = nc * SPLIT
    heads = width // HEAD
    levels = tm_size.bit_length() - 1
    first = slot == 0

    loads = [
        pltpu.make_async_copy(
            w_hbm.at[j], wbuf.at[pl.ds(j * full, full)], load_sem.at[j]
        )
        for j in range(3)
    ]
    loads.append(pltpu.make_async_copy(wo_hbm, wo, load_sem.at[3]))
    loads.append(pltpu.make_async_copy(noise_hbm, noise, load_sem.at[4]))

    def crows(c, base=0):
        return pl.ds(pl.multiple_of(base + c * chunk, 16), chunk)

    def srows(c):
        return pl.ds(pl.multiple_of(c * sub, 16), sub)

    partners = []
    for k in range(levels):
        bit = lax.rem(slot // (1 << k), 2)
        partners.append((slot + (1 - 2 * bit) * (1 << k), bit))

    barrier = pltpu.get_barrier_semaphore()
    for d in range(1, n):
        pl.semaphore_signal(
            barrier, inc=1, device_id={"tensor": lax.rem(z + d, n)},
            device_id_type=pl.DeviceIdType.MESH,
        )
    for partner, _ in partners:
        pl.semaphore_signal(
            barrier, inc=1, device_id={"tm": partner},
            device_id_type=pl.DeviceIdType.MESH,
        )

    gat[z, pl.ds(0, HDR), :] = mod_ref[...].astype(bf16)

    def cast(c, carry):
        gat[z, crows(c, HDR), :] = x_ref[crows(c), :].astype(bf16)
        return carry

    lax.fori_loop(0, nc, cast, 0)
    pl.semaphore_wait(barrier, n - 1 + levels)

    right = jnp.minimum(z + 1, n - 1)
    left = jnp.maximum(z - 1, 0)

    def ag(s, c, way):
        rows = pl.ds(0, HDR) if c is None else crows(c, HDR)
        i = nc if c is None else c
        return pltpu.make_async_remote_copy(
            src_ref=gat.at[s, rows], dst_ref=gat.at[s, rows],
            send_sem=ag_send.at[way, s, i], recv_sem=ag_recv.at[s, i],
            device_id={"tensor": right if way == 0 else left},
            device_id_type=pl.DeviceIdType.MESH,
        )

    def own(c):
        @pl.when(z < n - 1)
        def _():
            ag(z, c, 0).start()

        @pl.when(z > 0)
        def _():
            ag(z, c, 1).start()

    def forward(d, c):
        @pl.when(z >= d)
        def _():
            ag(z - d, c, 0).wait_recv()

            @pl.when(z < n - 1)
            def _():
                ag(z - d, c, 0).start()

        @pl.when(z + d < n)
        def _():
            ag(z + d, c, 1).wait_recv()

            @pl.when(z > 0)
            def _():
                ag(z + d, c, 1).start()

    for load in loads:
        load.start()

    even = partners[0][1] == 0

    @pl.when(jnp.logical_not(even))
    def _():
        pl.semaphore_wait(gate, 1)

    own(None)

    def own_loop(c, carry):
        own(c)
        return carry

    lax.fori_loop(0, nc, own_loop, 0)

    def drain_gather():
        def one(c, carry):
            drain_one(c)
            return carry

        drain_one(None)
        lax.fori_loop(0, nc, one, 0)

    def drain_one(c):
        for s in range(n):
            @pl.when((z < n - 1) & (s <= z))
            def _():
                ag(s, c, 0).wait_send()

            @pl.when((z > 0) & (s >= z))
            def _():
                ag(s, c, 1).wait_send()

    for d in range(1, n):
        forward(d, None)
        if d < n - 1:

            def forward_loop(c, carry, d=d):
                forward(d, c)
                return carry

            lax.fori_loop(0, nc, forward_loop, 0)

    for load in loads:
        load.wait()

    def project(c, carry):
        forward(n - 1, c)

        @pl.when((c == nc - 1) & even)
        def _():
            drain_gather()
            pl.semaphore_signal(
                gate, inc=1, device_id={"tm": partners[0][0]},
                device_id_type=pl.DeviceIdType.MESH,
            )

        rows = crows(c, HDR)
        total = jnp.zeros((chunk, 1), f32)
        square = jnp.zeros((chunk, 1), f32)
        for s in range(n):
            part = gat[s, rows, :].astype(f32)
            total += jnp.sum(part, axis=1, keepdims=True)
            square += jnp.sum(part * part, axis=1, keepdims=True)
        mean = total * (1.0 / full)
        var = square * (1.0 / full) - mean * mean
        rstd = lax.rsqrt(var + epsilon)
        for s in range(n):
            head_rows = gat[s, pl.ds(0, HDR), :].astype(f32)
            part = gat[s, rows, :].astype(f32)
            modb[:, s * width : (s + 1) * width] = (
                (part - mean) * rstd * (1.0 + head_rows[1:2]) + head_rows[0:1]
            ).astype(bf16)
        for j in range(3):
            out = jnp.dot(
                modb[...], wbuf[j * full : (j + 1) * full, :], preferred_element_type=f32
            )
            if j == 2:
                qkv[j, crows(c), :] = out.astype(bf16)
            else:
                for h in range(heads):
                    cols = slice(h * HEAD, (h + 1) * HEAD)
                    vec = out[:, cols]
                    power = jnp.mean(vec * vec, axis=1, keepdims=True)
                    qkv[j, crows(c), cols] = (
                        vec * lax.rsqrt(power + epsilon) * gains_ref[j : j + 1, cols]
                    ).astype(bf16)
        return carry

    lax.fori_loop(0, nc, project, 0)

    def prow(t, c):
        return pl.ds(pl.multiple_of(t * length + c * sub, 16), sub)

    def rs(t, c, way):
        if way == 0:
            place = t
        else:
            place = jnp.where(t == z - 1, n, t)
        return pltpu.make_async_remote_copy(
            src_ref=wbuf.at[prow(t, c)], dst_ref=rbuf.at[place, srows(c)],
            send_sem=rs_send.at[way, t, c], recv_sem=rs_recv.at[way, t, c],
            device_id={"tensor": right if way == 0 else left},
            device_id_type=pl.DeviceIdType.MESH,
        )

    def tx(k, c):
        return pltpu.make_async_remote_copy(
            src_ref=tsend.at[k, srows(c)], dst_ref=trecv.at[k, srows(c)],
            send_sem=t_send.at[k, c], recv_sem=t_recv.at[k, c],
            device_id={"tm": partners[k][0]}, device_id_type=pl.DeviceIdType.MESH,
        )

    exponent = math.log2(math.e) / math.sqrt(HEAD)

    def stage_attend(c):
        def one_head(h, carry):
            cols = pl.ds(pl.multiple_of(h * HEAD, HEAD), HEAD)
            scores = lax.dot_general(
                qkv[0, crows(c), cols], qkv[1, :, cols], (((1,), (1,)), ((), ())),
                preferred_element_type=f32,
            )
            top = jnp.max(scores, axis=1, keepdims=True)
            weights = jnp.exp2((scores - top) * exponent)
            norm = jnp.sum(weights, axis=1, keepdims=True)
            out = jnp.dot(weights.astype(bf16), qkv[2, :, cols], preferred_element_type=f32)
            att[:, cols] = (out / norm).astype(bf16)
            return carry

        lax.fori_loop(0, heads, one_head, 0, unroll=3)

        def one_part(t, carry):
            cols = pl.ds(pl.multiple_of(t * width, 128), width)
            part = jnp.dot(att[...], wo[:, cols], preferred_element_type=f32)
            wbuf[pl.ds(pl.multiple_of(t * length + c * chunk, 16), chunk), :] = part.astype(
                bf16
            )
            return carry

        lax.fori_loop(0, n, one_part, 0)

        @pl.when(z == 0)
        def _():
            for p in range(SPLIT):
                for t in range(n - 1, 0, -1):
                    rs(t, c * SPLIT + p, 0).start()

        @pl.when(z == n - 1)
        def _():
            for p in range(SPLIT):
                for t in range(n - 1):
                    rs(t, c * SPLIT + p, 1).start()

    def stage_join(c):
        for t in range(n - 1, 0, -1):
            @pl.when((z > 0) & (z < t))
            def _():
                rs(t, c, 0).wait_recv()
                wbuf[prow(t, c), :] = (
                    wbuf[prow(t, c), :].astype(f32) + rbuf[t, srows(c), :].astype(f32)
                ).astype(bf16)
                rs(t, c, 0).start()

            u = n - 1 - t

            @pl.when((z < n - 1) & (z > u))
            def _():
                rs(u, c, 1).wait_recv()
                wbuf[prow(u, c), :] = (
                    wbuf[prow(u, c), :].astype(f32) + rbuf[u, srows(c), :].astype(f32)
                ).astype(bf16)
                rs(u, c, 1).start()

    def stage_velocity(c):
        rows = srows(c)

        @pl.when(z > 0)
        def _():
            rs(z, c, 0).wait_recv()

        @pl.when(z < n - 1)
        def _():
            pltpu.make_async_remote_copy(
                src_ref=wbuf.at[prow(z, c)], dst_ref=rbuf.at[n, rows],
                send_sem=rs_send.at[1, z, c], recv_sem=rs_recv.at[1, z, c],
                device_id={"tensor": right}, device_id_type=pl.DeviceIdType.MESH,
            ).wait_recv()

        branch = wbuf[prow(z, c), :].astype(f32)
        upd_ref[rows, :] = branch

        @pl.when(z > 0)
        def _():
            upd_ref[rows, :] = upd_ref[rows, :] + rbuf[z, rows, :].astype(f32)

        @pl.when(z < n - 1)
        def _():
            upd_ref[rows, :] = upd_ref[rows, :] + rbuf[n, rows, :].astype(f32)

        state = x_ref[rows, :]
        velocity = state + mod_ref[2:3, :] * upd_ref[rows, :]
        vel_ref[rows, :] = velocity.astype(bf16)
        start = jnp.where(first, state, jnp.zeros_like(state))
        upd_ref[rows, :] = start
        tsend[0, rows, :] = (
            noise[rows, :].astype(f32) - step_ref[0] * velocity + start
        ).astype(bf16)
        tx(0, c).start()

    def stage_prefix(k, c):
        rows = srows(c)
        tx(k, c).wait_recv()
        arrived = trecv[k, rows, :].astype(f32)
        if k < levels - 1:
            tsend[k + 1, rows, :] = (tsend[k, rows, :].astype(f32) + arrived).astype(bf16)
            tx(k + 1, c).start()
        keep = partners[k][1].astype(f32)
        now = upd_ref[rows, :] + keep * arrived
        upd_ref[rows, :] = now
        if k == levels - 1:
            change = now - x_ref[rows, :]
            erracc[...] += jnp.sum(
                (change * change).reshape(sub // 8, 8, width), axis=0
            )

    erracc[...] = jnp.zeros_like(erracc)
    lag = 5

    def turn(i, carry):
        @pl.when((i < ns) & (lax.rem(i, SPLIT) == 0))
        def _():
            stage_attend(i // SPLIT)

        @pl.when((i >= 1) & (i < ns + 1))
        def _():
            stage_join(i - 1)

        @pl.when((i >= lag) & (i < ns + lag))
        def _():
            stage_velocity(i - lag)

        for k in range(levels):
            @pl.when((i >= lag + 1 + k) & (i < ns + lag + 1 + k))
            def _(k=k):
                stage_prefix(k, i - (lag + 1 + k))

        return carry

    lax.fori_loop(0, ns + lag + levels, turn, 0)

    ebuf[z] = jnp.zeros((8, 128), f32) + jnp.sum(erracc[...])

    def ex(d):
        return pltpu.make_async_remote_copy(
            src_ref=ebuf.at[z], dst_ref=ebuf.at[z],
            send_sem=e_send.at[d], recv_sem=e_recv.at[d],
            device_id={"tensor": lax.rem(z + d, n)}, device_id_type=pl.DeviceIdType.MESH,
        )

    for d in range(1, n):
        ex(d).start()

    @pl.when(jnp.logical_not(even))
    def _():
        drain_gather()

    def drain(c, carry):
        for s in range(n):
            @pl.when(z < s)
            def _():
                rs(s, c, 0).wait_send()

            @pl.when(z > s)
            def _():
                rs(s, c, 1).wait_send()

        for k in range(levels):
            tx(k, c).wait_send()
        return carry

    lax.fori_loop(0, ns, drain, 0)
    for d in range(1, n):
        ex(d).wait()
    total = ebuf[0]
    for s in range(1, n):
        total = total + ebuf[s]
    err_ref[...] = total


def body(latents, noise, qkv_weight, qk_gains, out_weight, modulation, step_sizes, window_start):
    n = lax.axis_size("tensor")
    tm_size = lax.axis_size("tm")
    offset = window_start[0] + lax.axis_index("tm")
    _, length, width = latents.shape
    full = n * width
    mod_rows = lax.dynamic_index_in_dim(
        modulation.transpose(1, 0, 2), offset, 1, keepdims=False
    ).astype(f32)
    mod_rows = jnp.pad(mod_rows, ((0, HDR - 3), (0, 0)))
    step_size = lax.dynamic_slice_in_dim(step_sizes, offset, 1, 0)
    chunk = CHUNK
    nc = length // chunk
    ns = nc * SPLIT
    levels = tm_size.bit_length() - 1
    vmem = pl.BlockSpec(memory_space=pltpu.VMEM)
    hbm = pl.BlockSpec(memory_space=pl.ANY)
    dma = pltpu.SemaphoreType.DMA
    updated, velocity, err = pl.pallas_call(
        functools.partial(kernel, n, tm_size, chunk),
        out_shape=(
            jax.ShapeDtypeStruct((length, width), f32),
            jax.ShapeDtypeStruct((length, width), bf16),
            jax.ShapeDtypeStruct((8, 128), f32),
        ),
        in_specs=[vmem, hbm, hbm, vmem, hbm, vmem, pl.BlockSpec(memory_space=pltpu.SMEM)],
        out_specs=(vmem, vmem, vmem),
        scratch_shapes=[
            pltpu.VMEM((n, HDR + length, width), bf16),
            pltpu.VMEM((3 * full, width), bf16),
            pltpu.VMEM((width, full), bf16),
            pltpu.VMEM((3, length, width), bf16),
            pltpu.VMEM((n + 1, length, width), bf16),
            pltpu.VMEM((levels, length, width), bf16),
            pltpu.VMEM((levels, length, width), bf16),
            pltpu.VMEM((length, width), bf16),
            pltpu.VMEM((chunk, full), bf16),
            pltpu.VMEM((chunk, width), bf16),
            pltpu.VMEM((8, width), f32),
            pltpu.VMEM((n, 8, 128), f32),
            dma((5,)),
            dma((2, n, nc + 1)),
            dma((n, nc + 1)),
            dma((2, n, ns)),
            dma((2, n, ns)),
            dma((levels, ns)),
            dma((levels, ns)),
            dma((n,)),
            dma((n,)),
            pltpu.SemaphoreType.REGULAR,
        ],
        compiler_params=pltpu.CompilerParams(
            collective_id=0, has_side_effects=True, vmem_limit_bytes=62 * 2**20
        ),
    )(
        latents[0], noise[0], qkv_weight.transpose(1, 0, 2), qk_gains, out_weight,
        mod_rows, step_size,
    )
    return (updated[None], velocity[None], err[0, :1] / (length * full))


def solution(mesh):
    return jax.shard_map(
        body,
        mesh=mesh,
        in_specs=(
            P("tm", None, "tensor"),
            P("tm", None, "tensor"),
            P(None, None, "tensor"),
            P(None, "tensor"),
            P("tensor", None),
            P(None, None, "tensor"),
            P(),
            P(),
        ),
        out_specs=(P("tm", None, "tensor"), P("tm", None, "tensor"), P("tm")),
        check_vma=False,
    )
```

```python
import functools
import math

import jax
import jax.numpy as jnp
from jax import lax
from jax.experimental import pallas as pl
from jax.experimental.pallas import tpu as pltpu
from jax.sharding import PartitionSpec as P

HEAD = 128
HDR = 16
CHUNK = 256
SPLIT = 2
epsilon = 1e-06
f32 = jnp.float32
bf16 = jnp.bfloat16


def kernel(
    n, tm_size, chunk,
    x_ref, noise_hbm, w_hbm, gains_ref, wo_hbm, mod_ref, step_ref,
    upd_ref, vel_ref, err_ref,
    gat, wbuf, wo, qkv, rbuf, trecv, noise, acc, att, erracc, ebuf, sums, stat,
    load_sem, ag_send, ag_recv, rs_send, rs_recv, t_send, t_recv, e_send, e_recv,
    s_send, s_recv, gate,
):
    z = lax.axis_index("tensor")
    slot = lax.axis_index("tm")
    length, width = x_ref.shape
    full = n * width
    nc = length // chunk
    sub = chunk // SPLIT
    ns = nc * SPLIT
    heads = width // HEAD
    levels = tm_size.bit_length() - 1
    first = slot == 0

    loads = [
        pltpu.make_async_copy(
            w_hbm.at[j], wbuf.at[pl.ds(j * full, full)], load_sem.at[j]
        )
        for j in range(3)
    ]
    loads.append(pltpu.make_async_copy(wo_hbm, wo, load_sem.at[3]))
    loads.append(pltpu.make_async_copy(noise_hbm, noise, load_sem.at[4]))

    def crows(c, base=0):
        return pl.ds(pl.multiple_of(base + c * chunk, 16), chunk)

    def srows(c):
        return pl.ds(pl.multiple_of(c * sub, 16), sub)

    partners = []
    for k in range(levels):
        bit = lax.rem(slot // (1 << k), 2)
        partners.append((slot + (1 - 2 * bit) * (1 << k), bit))

    barrier = pltpu.get_barrier_semaphore()
    for d in range(1, n):
        pl.semaphore_signal(
            barrier, inc=1, device_id={"tensor": lax.rem(z + d, n)},
            device_id_type=pl.DeviceIdType.MESH,
        )
    for partner, _ in partners:
        pl.semaphore_signal(
            barrier, inc=1, device_id={"tm": partner},
            device_id_type=pl.DeviceIdType.MESH,
        )

    for load in loads:
        load.start()

    gat[z, pl.ds(0, HDR), :] = mod_ref[...].astype(bf16)

    def cast(c, carry):
        gat[z, crows(c, HDR), :] = x_ref[crows(c), :].astype(bf16)
        return carry

    lax.fori_loop(0, nc, cast, 0)
    pl.semaphore_wait(barrier, n - 1 + levels)

    right = jnp.minimum(z + 1, n - 1)
    left = jnp.maximum(z - 1, 0)

    def ag(s, c, way):
        rows = pl.ds(0, HDR) if c is None else crows(c, HDR)
        i = nc if c is None else c
        return pltpu.make_async_remote_copy(
            src_ref=gat.at[s, rows], dst_ref=gat.at[s, rows],
            send_sem=ag_send.at[way, s, i], recv_sem=ag_recv.at[s, i],
            device_id={"tensor": right if way == 0 else left},
            device_id_type=pl.DeviceIdType.MESH,
        )

    def own(c):
        @pl.when(z < n - 1)
        def _():
            ag(z, c, 0).start()

        @pl.when(z > 0)
        def _():
            ag(z, c, 1).start()

    def forward(d, c):
        @pl.when(z >= d)
        def _():
            ag(z - d, c, 0).wait_recv()

            @pl.when(z < n - 1)
            def _():
                ag(z - d, c, 0).start()

        @pl.when(z + d < n)
        def _():
            ag(z + d, c, 1).wait_recv()

            @pl.when(z > 0)
            def _():
                ag(z + d, c, 1).start()

    even = partners[0][1] == 0

    def own_all():
        own(None)

        def own_loop(c, carry):
            own(c)
            return carry

        lax.fori_loop(0, nc, own_loop, 0)

    @pl.when(even)
    def _():
        own_all()

    ones = jnp.ones((8, width), bf16)

    def row_sum(rows):
        return lax.dot_general(
            ones, rows, (((1,), (1,)), ((), ())), preferred_element_type=f32
        )

    def count(c, carry):
        part = gat[z, crows(c, HDR), :]
        square = part.astype(f32) * part.astype(f32)
        high = square.astype(bf16)
        low = (square - high.astype(f32)).astype(bf16)
        lanes = pl.ds(pl.multiple_of(c * chunk, 128), chunk)
        sums[z, 0:8, lanes] = row_sum(part)
        sums[z, 8:16, lanes] = row_sum(high) + row_sum(low)
        return carry

    lax.fori_loop(0, nc, count, 0)

    def sx(d):
        return pltpu.make_async_remote_copy(
            src_ref=sums.at[z], dst_ref=sums.at[z],
            send_sem=s_send.at[d], recv_sem=s_recv.at[d],
            device_id={"tensor": lax.rem(z + d, n)}, device_id_type=pl.DeviceIdType.MESH,
        )

    for d in range(1, n):
        sx(d).start()

    def drain_gather():
        def one(c, carry):
            drain_one(c)
            return carry

        drain_one(None)
        lax.fori_loop(0, nc, one, 0)

    def drain_one(c):
        for s in range(n):
            @pl.when((z < n - 1) & (s <= z))
            def _():
                ag(s, c, 0).wait_send()

            @pl.when((z > 0) & (s >= z))
            def _():
                ag(s, c, 1).wait_send()

    for load in loads:
        load.wait()
    for d in range(1, n):
        sx(d).wait()

    total = sums[0]
    for s in range(1, n):
        total = total + sums[s]
    mean_row = total[0:8] * (1.0 / full)
    stat[0:8, :] = mean_row
    stat[8:16, :] = lax.rsqrt(total[8:16] * (1.0 / full) - mean_row * mean_row + epsilon)

    def accumulate(s, c, begin):
        lanes = pl.ds(pl.multiple_of(c * chunk, 128), chunk)
        columns = jnp.transpose(stat[:, lanes])
        head_rows = gat[s, pl.ds(0, HDR), :].astype(f32)
        part = gat[s, crows(c, HDR), :].astype(f32)
        rows = (
            (part - columns[:, 0:1]) * columns[:, 8:9] * (1.0 + head_rows[1:2]) + head_rows[0:1]
        ).astype(bf16)
        for j in range(3):
            cols = slice(j * width, (j + 1) * width)
            depth = pl.ds(pl.multiple_of(j * full + s * width, 128), width)
            out = jnp.dot(rows, wbuf[depth, :], preferred_element_type=f32)
            if begin:
                acc[crows(c), cols] = out
            else:
                acc[crows(c), cols] += out

    def own_part(c, carry):
        accumulate(z, c, True)
        return carry

    lax.fori_loop(0, nc, own_part, 0)

    @pl.when(jnp.logical_not(even))
    def _():
        pl.semaphore_wait(gate, 1)
        own_all()

    def finish(c):
        for j in range(3):
            for h in range(heads):
                cols = slice(h * HEAD, (h + 1) * HEAD)
                vec = acc[crows(c), j * width + h * HEAD : j * width + (h + 1) * HEAD]
                if j < 2:
                    power = jnp.mean(vec * vec, axis=1, keepdims=True)
                    vec = vec * lax.rsqrt(power + epsilon) * gains_ref[j : j + 1, cols]
                qkv[j, crows(c), cols] = vec.astype(bf16)

    def distance(d, carry):
        forward(d, None)

        def one(c, carry):
            forward(d, c)

            @pl.when((d == n - 1) & (c == 0) & even)
            def _():
                drain_gather()
                pl.semaphore_signal(
                    gate, inc=1, device_id={"tm": partners[0][0]},
                    device_id_type=pl.DeviceIdType.MESH,
                )

            @pl.when(z >= d)
            def _():
                accumulate(z - d, c, False)

            @pl.when(z + d < n)
            def _():
                accumulate(z + d, c, False)

            @pl.when(d == n - 1)
            def _():
                finish(c)

            return carry

        lax.fori_loop(0, nc, one, 0)
        return carry

    lax.fori_loop(1, n, distance, 0)

    def prow(t, c):
        return pl.ds(pl.multiple_of(t * length + c * sub, 16), sub)

    def rs(t, c, way):
        if way == 0:
            place = t
        else:
            place = jnp.where(t == z - 1, n, t)
        return pltpu.make_async_remote_copy(
            src_ref=wbuf.at[prow(t, c)], dst_ref=rbuf.at[place, srows(c)],
            send_sem=rs_send.at[way, t, c], recv_sem=rs_recv.at[way, t, c],
            device_id={"tensor": right if way == 0 else left},
            device_id_type=pl.DeviceIdType.MESH,
        )

    def tx(k, c):
        return pltpu.make_async_remote_copy(
            src_ref=wbuf.at[prow(n + k, c)], dst_ref=trecv.at[k, srows(c)],
            send_sem=t_send.at[k, c], recv_sem=t_recv.at[k, c],
            device_id={"tm": partners[k][0]}, device_id_type=pl.DeviceIdType.MESH,
        )

    exponent = math.log2(math.e) / math.sqrt(HEAD)

    def stage_attend(c):
        def one_head(h, carry):
            cols = pl.ds(pl.multiple_of(h * HEAD, HEAD), HEAD)
            scores = lax.dot_general(
                qkv[0, crows(c), cols], qkv[1, :, cols], (((1,), (1,)), ((), ())),
                preferred_element_type=f32,
            )
            top = jnp.max(scores, axis=1, keepdims=True)
            weights = jnp.exp2((scores - top) * exponent)
            norm = jnp.sum(weights, axis=1, keepdims=True)
            out = jnp.dot(weights.astype(bf16), qkv[2, :, cols], preferred_element_type=f32)
            att[:, cols] = (out / norm).astype(bf16)
            return carry

        lax.fori_loop(0, heads, one_head, 0, unroll=3)

        def one_part(t, carry):
            cols = pl.ds(pl.multiple_of(t * width, 128), width)
            part = jnp.dot(att[...], wo[:, cols], preferred_element_type=f32)
            wbuf[pl.ds(pl.multiple_of(t * length + c * chunk, 16), chunk), :] = part.astype(
                bf16
            )
            return carry

        lax.fori_loop(0, n, one_part, 0)

        @pl.when(z == 0)
        def _():
            for p in range(SPLIT):
                for t in range(n - 1, 0, -1):
                    rs(t, c * SPLIT + p, 0).start()

        @pl.when(z == n - 1)
        def _():
            for p in range(SPLIT):
                for t in range(n - 1):
                    rs(t, c * SPLIT + p, 1).start()

    def stage_join(c):
        for t in range(n - 1, 0, -1):
            @pl.when((z > 0) & (z < t))
            def _():
                rs(t, c, 0).wait_recv()
                wbuf[prow(t, c), :] = (
                    wbuf[prow(t, c), :].astype(f32) + rbuf[t, srows(c), :].astype(f32)
                ).astype(bf16)
                rs(t, c, 0).start()

            u = n - 1 - t

            @pl.when((z < n - 1) & (z > u))
            def _():
                rs(u, c, 1).wait_recv()
                wbuf[prow(u, c), :] = (
                    wbuf[prow(u, c), :].astype(f32) + rbuf[u, srows(c), :].astype(f32)
                ).astype(bf16)
                rs(u, c, 1).start()

    def stage_velocity(c):
        rows = srows(c)

        @pl.when(z > 0)
        def _():
            rs(z, c, 0).wait_recv()

        @pl.when(z < n - 1)
        def _():
            pltpu.make_async_remote_copy(
                src_ref=wbuf.at[prow(z, c)], dst_ref=rbuf.at[n, rows],
                send_sem=rs_send.at[1, z, c], recv_sem=rs_recv.at[1, z, c],
                device_id={"tensor": right}, device_id_type=pl.DeviceIdType.MESH,
            ).wait_recv()

        branch = wbuf[prow(z, c), :].astype(f32)
        upd_ref[rows, :] = branch

        @pl.when(z > 0)
        def _():
            upd_ref[rows, :] = upd_ref[rows, :] + rbuf[z, rows, :].astype(f32)

        @pl.when(z < n - 1)
        def _():
            upd_ref[rows, :] = upd_ref[rows, :] + rbuf[n, rows, :].astype(f32)

        state = x_ref[rows, :]
        velocity = state + mod_ref[2:3, :] * upd_ref[rows, :]
        vel_ref[rows, :] = velocity.astype(bf16)
        start = jnp.where(first, state, jnp.zeros_like(state))
        upd_ref[rows, :] = start
        wbuf[prow(n, c), :] = (
            noise[rows, :].astype(f32) - step_ref[0] * velocity + start
        ).astype(bf16)
        tx(0, c).start()

    def stage_prefix(k, c):
        rows = srows(c)
        tx(k, c).wait_recv()
        arrived = trecv[k, rows, :].astype(f32)
        if k < levels - 1:
            wbuf[prow(n + k + 1, c), :] = (
                wbuf[prow(n + k, c), :].astype(f32) + arrived
            ).astype(bf16)
            tx(k + 1, c).start()
        keep = partners[k][1].astype(f32)
        now = upd_ref[rows, :] + keep * arrived
        upd_ref[rows, :] = now
        if k == levels - 1:
            change = now - x_ref[rows, :]
            erracc[...] += jnp.sum(
                (change * change).reshape(sub // 8, 8, width), axis=0
            )

    erracc[...] = jnp.zeros_like(erracc)
    lag = 5

    def turn(i, carry):
        @pl.when((i < ns) & (lax.rem(i, SPLIT) == 0))
        def _():
            stage_attend(i // SPLIT)

        @pl.when((i >= 1) & (i < ns + 1))
        def _():
            stage_join(i - 1)

        @pl.when((i >= lag) & (i < ns + lag))
        def _():
            stage_velocity(i - lag)

        for k in range(levels):
            @pl.when((i >= lag + 1 + k) & (i < ns + lag + 1 + k))
            def _(k=k):
                stage_prefix(k, i - (lag + 1 + k))

        return carry

    lax.fori_loop(0, ns + lag + levels, turn, 0)

    ebuf[z] = jnp.zeros((8, 128), f32) + jnp.sum(erracc[...])

    def ex(d):
        return pltpu.make_async_remote_copy(
            src_ref=ebuf.at[z], dst_ref=ebuf.at[z],
            send_sem=e_send.at[d], recv_sem=e_recv.at[d],
            device_id={"tensor": lax.rem(z + d, n)}, device_id_type=pl.DeviceIdType.MESH,
        )

    for d in range(1, n):
        ex(d).start()

    @pl.when(jnp.logical_not(even))
    def _():
        drain_gather()

    def drain(c, carry):
        for s in range(n):
            @pl.when(z < s)
            def _():
                rs(s, c, 0).wait_send()

            @pl.when(z > s)
            def _():
                rs(s, c, 1).wait_send()

        for k in range(levels):
            tx(k, c).wait_send()
        return carry

    lax.fori_loop(0, ns, drain, 0)
    for d in range(1, n):
        ex(d).wait()
    total = ebuf[0]
    for s in range(1, n):
        total = total + ebuf[s]
    err_ref[...] = total


def body(latents, noise, qkv_weight, qk_gains, out_weight, modulation, step_sizes, window_start):
    n = lax.axis_size("tensor")
    tm_size = lax.axis_size("tm")
    offset = window_start[0] + lax.axis_index("tm")
    _, length, width = latents.shape
    full = n * width
    mod_rows = lax.dynamic_index_in_dim(
        modulation.transpose(1, 0, 2), offset, 1, keepdims=False
    ).astype(f32)
    mod_rows = jnp.pad(mod_rows, ((0, HDR - 3), (0, 0)))
    step_size = lax.dynamic_slice_in_dim(step_sizes, offset, 1, 0)
    chunk = CHUNK
    nc = length // chunk
    ns = nc * SPLIT
    levels = tm_size.bit_length() - 1
    vmem = pl.BlockSpec(memory_space=pltpu.VMEM)
    hbm = pl.BlockSpec(memory_space=pl.ANY)
    dma = pltpu.SemaphoreType.DMA
    updated, velocity, err = pl.pallas_call(
        functools.partial(kernel, n, tm_size, chunk),
        out_shape=(
            jax.ShapeDtypeStruct((length, width), f32),
            jax.ShapeDtypeStruct((length, width), bf16),
            jax.ShapeDtypeStruct((8, 128), f32),
        ),
        in_specs=[vmem, hbm, hbm, vmem, hbm, vmem, pl.BlockSpec(memory_space=pltpu.SMEM)],
        out_specs=(vmem, vmem, vmem),
        scratch_shapes=[
            pltpu.VMEM((n, HDR + length, width), bf16),
            pltpu.VMEM((max(3 * full, (n + levels) * length), width), bf16),
            pltpu.VMEM((width, full), bf16),
            pltpu.VMEM((3, length, width), bf16),
            pltpu.VMEM((n + 1, length, width), bf16),
            pltpu.VMEM((levels, length, width), bf16),
            pltpu.VMEM((length, width), bf16),
            pltpu.VMEM((length, 3 * width), f32),
            pltpu.VMEM((chunk, width), bf16),
            pltpu.VMEM((8, width), f32),
            pltpu.VMEM((n, 8, 128), f32),
            pltpu.VMEM((n, 16, length), f32),
            pltpu.VMEM((16, length), f32),
            dma((5,)),
            dma((2, n, nc + 1)),
            dma((n, nc + 1)),
            dma((2, n, ns)),
            dma((2, n, ns)),
            dma((levels, ns)),
            dma((levels, ns)),
            dma((n,)),
            dma((n,)),
            dma((n,)),
            dma((n,)),
            pltpu.SemaphoreType.REGULAR,
        ],
        compiler_params=pltpu.CompilerParams(
            collective_id=0, has_side_effects=True, vmem_limit_bytes=62 * 2**20
        ),
    )(
        latents[0], noise[0], qkv_weight.transpose(1, 0, 2), qk_gains, out_weight,
        mod_rows, step_size,
    )
    return (updated[None], velocity[None], err[0, :1] / (length * full))


def solution(mesh):
    return jax.shard_map(
        body,
        mesh=mesh,
        in_specs=(
            P("tm", None, "tensor"),
            P("tm", None, "tensor"),
            P(None, None, "tensor"),
            P(None, "tensor"),
            P("tensor", None),
            P(None, None, "tensor"),
            P(),
            P(),
        ),
        out_specs=(P("tm", None, "tensor"), P("tm", None, "tensor"), P("tm")),
        check_vma=False,
    )
```

```python
import functools
import math

import jax
import jax.numpy as jnp
from jax import lax
from jax.experimental import pallas as pl
from jax.experimental.pallas import tpu as pltpu
from jax.sharding import PartitionSpec as P

HEAD = 128
HDR = 16
CHUNK = 256
SPLIT = 2
epsilon = 1e-06
f32 = jnp.float32
bf16 = jnp.bfloat16


def kernel(
    n, tm_size, chunk,
    x_ref, noise_hbm, w_hbm, gains_ref, wo_hbm, mod_ref,
    upd_ref, vel_ref, err_ref,
    gat, wbuf, wo, qkv, rbuf, trecv, noise, acc, att, erracc, ebuf, sums, stat,
    load_sem, ag_send, ag_recv, rs_send, rs_recv, t_send, t_recv, e_send, e_recv,
    s_send, s_recv,
):
    z = lax.axis_index("tensor")
    slot = lax.axis_index("tm")
    length, width = x_ref.shape
    full = n * width
    nc = length // chunk
    sub = chunk // SPLIT
    ns = nc * SPLIT
    heads = width // HEAD
    levels = tm_size.bit_length() - 1
    first = slot == 0

    loads = [
        pltpu.make_async_copy(
            w_hbm.at[j], wbuf.at[pl.ds(j * full, full)], load_sem.at[j]
        )
        for j in range(3)
    ]
    loads.append(pltpu.make_async_copy(wo_hbm, wo, load_sem.at[3]))
    loads.append(pltpu.make_async_copy(noise_hbm, noise, load_sem.at[4]))

    def crows(c, base=0):
        return pl.ds(pl.multiple_of(base + c * chunk, 16), chunk)

    def srows(c):
        return pl.ds(pl.multiple_of(c * sub, 16), sub)

    partners = []
    for k in range(levels):
        bit = lax.rem(slot // (1 << k), 2)
        partners.append((slot + (1 - 2 * bit) * (1 << k), bit))

    barrier = pltpu.get_barrier_semaphore()
    for d in range(1, n):
        pl.semaphore_signal(
            barrier, inc=1, device_id={"tensor": lax.rem(z + d, n)},
            device_id_type=pl.DeviceIdType.MESH,
        )
    for partner, _ in partners:
        pl.semaphore_signal(
            barrier, inc=1, device_id={"tm": partner},
            device_id_type=pl.DeviceIdType.MESH,
        )

    for load in loads:
        load.start()

    gat[z, pl.ds(0, HDR), :] = mod_ref[...].astype(bf16)

    def cast(c, carry):
        gat[z, crows(c, HDR), :] = x_ref[crows(c), :].astype(bf16)
        return carry

    lax.fori_loop(0, nc, cast, 0)
    pl.semaphore_wait(barrier, n - 1 + levels)

    right = jnp.minimum(z + 1, n - 1)
    left = jnp.maximum(z - 1, 0)

    def ag(s, c, way):
        rows = pl.ds(0, HDR) if c is None else crows(c, HDR)
        i = nc if c is None else c
        return pltpu.make_async_remote_copy(
            src_ref=gat.at[s, rows], dst_ref=gat.at[s, rows],
            send_sem=ag_send.at[way, s, i], recv_sem=ag_recv.at[s, i],
            device_id={"tensor": right if way == 0 else left},
            device_id_type=pl.DeviceIdType.MESH,
        )

    def own(c):
        @pl.when(z < n - 1)
        def _():
            ag(z, c, 0).start()

        @pl.when(z > 0)
        def _():
            ag(z, c, 1).start()

    def forward(d, c):
        @pl.when(z >= d)
        def _():
            ag(z - d, c, 0).wait_recv()

            @pl.when(z < n - 1)
            def _():
                ag(z - d, c, 0).start()

        @pl.when(z + d < n)
        def _():
            ag(z + d, c, 1).wait_recv()

            @pl.when(z > 0)
            def _():
                ag(z + d, c, 1).start()

    def own_all():
        own(None)

        def own_loop(c, carry):
            own(c)
            return carry

        lax.fori_loop(0, nc, own_loop, 0)

    own_all()

    ones = jnp.ones((8, width), bf16)

    def row_sum(rows):
        return lax.dot_general(
            ones, rows, (((1,), (1,)), ((), ())), preferred_element_type=f32
        )

    def count(c, carry):
        part = gat[z, crows(c, HDR), :]
        square = part.astype(f32) * part.astype(f32)
        high = square.astype(bf16)
        low = (square - high.astype(f32)).astype(bf16)
        lanes = pl.ds(pl.multiple_of(c * chunk, 128), chunk)
        sums[z, 0:8, lanes] = row_sum(part)
        sums[z, 8:16, lanes] = row_sum(high) + row_sum(low)
        return carry

    lax.fori_loop(0, nc, count, 0)

    def sx(d):
        return pltpu.make_async_remote_copy(
            src_ref=sums.at[z], dst_ref=sums.at[z],
            send_sem=s_send.at[d], recv_sem=s_recv.at[d],
            device_id={"tensor": lax.rem(z + d, n)}, device_id_type=pl.DeviceIdType.MESH,
        )

    for d in range(1, n):
        sx(d).start()

    def drain_gather():
        def one(c, carry):
            drain_one(c)
            return carry

        drain_one(None)
        lax.fori_loop(0, nc, one, 0)

    def drain_one(c):
        for s in range(n):
            @pl.when((z < n - 1) & (s <= z))
            def _():
                ag(s, c, 0).wait_send()

            @pl.when((z > 0) & (s >= z))
            def _():
                ag(s, c, 1).wait_send()

    for load in loads:
        load.wait()
    for d in range(1, n):
        sx(d).wait()

    total = sums[0]
    for s in range(1, n):
        total = total + sums[s]
    mean_row = total[0:8] * (1.0 / full)
    stat[0:8, :] = mean_row
    stat[8:16, :] = lax.rsqrt(total[8:16] * (1.0 / full) - mean_row * mean_row + epsilon)

    def accumulate(s, c, begin):
        lanes = pl.ds(pl.multiple_of(c * chunk, 128), chunk)
        columns = jnp.transpose(stat[:, lanes])
        head_rows = gat[s, pl.ds(0, HDR), :].astype(f32)
        part = gat[s, crows(c, HDR), :].astype(f32)
        rows = (
            (part - columns[:, 0:1]) * columns[:, 8:9] * (1.0 + head_rows[1:2]) + head_rows[0:1]
        ).astype(bf16)
        for j in range(3):
            cols = slice(j * width, (j + 1) * width)
            depth = pl.ds(pl.multiple_of(j * full + s * width, 128), width)
            out = jnp.dot(rows, wbuf[depth, :], preferred_element_type=f32)
            if begin:
                acc[crows(c), cols] = out
            else:
                acc[crows(c), cols] += out

    def own_part(c, carry):
        accumulate(z, c, True)
        return carry

    lax.fori_loop(0, nc, own_part, 0)

    def finish(c):
        for j in range(3):
            for h in range(heads):
                cols = slice(h * HEAD, (h + 1) * HEAD)
                vec = acc[crows(c), j * width + h * HEAD : j * width + (h + 1) * HEAD]
                if j < 2:
                    power = jnp.mean(vec * vec, axis=1, keepdims=True)
                    vec = vec * lax.rsqrt(power + epsilon) * gains_ref[j : j + 1, cols]
                qkv[j, crows(c), cols] = vec.astype(bf16)

    def distance(d, carry):
        forward(d, None)

        def one(c, carry):
            forward(d, c)

            @pl.when(z >= d)
            def _():
                accumulate(z - d, c, False)

            @pl.when(z + d < n)
            def _():
                accumulate(z + d, c, False)

            @pl.when(d == n - 1)
            def _():
                finish(c)

            return carry

        lax.fori_loop(0, nc, one, 0)
        return carry

    lax.fori_loop(1, n, distance, 0)

    def prow(t, c):
        return pl.ds(pl.multiple_of(t * length + c * sub, 16), sub)

    def rs(t, c, way):
        if way == 0:
            place = t
        else:
            place = jnp.where(t == z - 1, n, t)
        return pltpu.make_async_remote_copy(
            src_ref=wbuf.at[prow(t, c)], dst_ref=rbuf.at[place, srows(c)],
            send_sem=rs_send.at[way, t, c], recv_sem=rs_recv.at[way, t, c],
            device_id={"tensor": right if way == 0 else left},
            device_id_type=pl.DeviceIdType.MESH,
        )

    def tx(k, c):
        return pltpu.make_async_remote_copy(
            src_ref=wbuf.at[prow(n + k, c)], dst_ref=trecv.at[k, srows(c)],
            send_sem=t_send.at[k, c], recv_sem=t_recv.at[k, c],
            device_id={"tm": partners[k][0]}, device_id_type=pl.DeviceIdType.MESH,
        )

    exponent = math.log2(math.e) / math.sqrt(HEAD)

    def stage_attend(c):
        def one_head(h, carry):
            cols = pl.ds(pl.multiple_of(h * HEAD, HEAD), HEAD)
            scores = lax.dot_general(
                qkv[0, crows(c), cols], qkv[1, :, cols], (((1,), (1,)), ((), ())),
                preferred_element_type=f32,
            )
            top = jnp.max(scores, axis=1, keepdims=True)
            weights = jnp.exp2((scores - top) * exponent)
            norm = jnp.sum(weights, axis=1, keepdims=True)
            out = jnp.dot(weights.astype(bf16), qkv[2, :, cols], preferred_element_type=f32)
            att[:, cols] = (out / norm).astype(bf16)
            return carry

        lax.fori_loop(0, heads, one_head, 0, unroll=3)

        def one_part(t, carry):
            cols = pl.ds(pl.multiple_of(t * width, 128), width)
            part = jnp.dot(att[...], wo[:, cols], preferred_element_type=f32)
            wbuf[pl.ds(pl.multiple_of(t * length + c * chunk, 16), chunk), :] = part.astype(
                bf16
            )
            return carry

        lax.fori_loop(0, n, one_part, 0)

        @pl.when(z == 0)
        def _():
            for p in range(SPLIT):
                for t in range(n - 1, 0, -1):
                    rs(t, c * SPLIT + p, 0).start()

        @pl.when(z == n - 1)
        def _():
            for p in range(SPLIT):
                for t in range(n - 1):
                    rs(t, c * SPLIT + p, 1).start()

    def stage_join(c):
        for t in range(n - 1, 0, -1):
            @pl.when((z > 0) & (z < t))
            def _():
                rs(t, c, 0).wait_recv()
                wbuf[prow(t, c), :] = (
                    wbuf[prow(t, c), :].astype(f32) + rbuf[t, srows(c), :].astype(f32)
                ).astype(bf16)
                rs(t, c, 0).start()

            u = n - 1 - t

            @pl.when((z < n - 1) & (z > u))
            def _():
                rs(u, c, 1).wait_recv()
                wbuf[prow(u, c), :] = (
                    wbuf[prow(u, c), :].astype(f32) + rbuf[u, srows(c), :].astype(f32)
                ).astype(bf16)
                rs(u, c, 1).start()

    def stage_velocity(c):
        rows = srows(c)

        @pl.when(z > 0)
        def _():
            rs(z, c, 0).wait_recv()

        @pl.when(z < n - 1)
        def _():
            pltpu.make_async_remote_copy(
                src_ref=wbuf.at[prow(z, c)], dst_ref=rbuf.at[n, rows],
                send_sem=rs_send.at[1, z, c], recv_sem=rs_recv.at[1, z, c],
                device_id={"tensor": right}, device_id_type=pl.DeviceIdType.MESH,
            ).wait_recv()

        branch = wbuf[prow(z, c), :].astype(f32)
        upd_ref[rows, :] = branch

        @pl.when(z > 0)
        def _():
            upd_ref[rows, :] = upd_ref[rows, :] + rbuf[z, rows, :].astype(f32)

        @pl.when(z < n - 1)
        def _():
            upd_ref[rows, :] = upd_ref[rows, :] + rbuf[n, rows, :].astype(f32)

        state = x_ref[rows, :]
        velocity = state + mod_ref[2:3, :] * upd_ref[rows, :]
        vel_ref[rows, :] = velocity.astype(bf16)
        start = jnp.where(first, state, jnp.zeros_like(state))
        upd_ref[rows, :] = start
        wbuf[prow(n, c), :] = (
            noise[rows, :].astype(f32) - mod_ref[3:4, :] * velocity + start
        ).astype(bf16)
        tx(0, c).start()

    def stage_prefix(k, c):
        rows = srows(c)
        tx(k, c).wait_recv()
        arrived = trecv[k, rows, :].astype(f32)
        if k < levels - 1:
            wbuf[prow(n + k + 1, c), :] = (
                wbuf[prow(n + k, c), :].astype(f32) + arrived
            ).astype(bf16)
            tx(k + 1, c).start()
        keep = partners[k][1].astype(f32)
        now = upd_ref[rows, :] + keep * arrived
        upd_ref[rows, :] = now
        if k == levels - 1:
            change = now - x_ref[rows, :]
            erracc[...] += jnp.sum(
                (change * change).reshape(sub // 8, 8, width), axis=0
            )

    erracc[...] = jnp.zeros_like(erracc)
    lag = 5

    def turn(i, carry):
        @pl.when((i < ns) & (lax.rem(i, SPLIT) == 0))
        def _():
            stage_attend(i // SPLIT)

        @pl.when((i >= 1) & (i < ns + 1))
        def _():
            stage_join(i - 1)

        @pl.when((i >= lag) & (i < ns + lag))
        def _():
            stage_velocity(i - lag)

        for k in range(levels):
            @pl.when((i >= lag + 1 + k) & (i < ns + lag + 1 + k))
            def _(k=k):
                stage_prefix(k, i - (lag + 1 + k))

        return carry

    lax.fori_loop(0, ns + lag + levels, turn, 0)

    ebuf[z] = jnp.zeros((8, 128), f32) + jnp.sum(erracc[...])

    def ex(d):
        return pltpu.make_async_remote_copy(
            src_ref=ebuf.at[z], dst_ref=ebuf.at[z],
            send_sem=e_send.at[d], recv_sem=e_recv.at[d],
            device_id={"tensor": lax.rem(z + d, n)}, device_id_type=pl.DeviceIdType.MESH,
        )

    for d in range(1, n):
        ex(d).start()

    drain_gather()

    def drain(c, carry):
        for s in range(n):
            @pl.when(z < s)
            def _():
                rs(s, c, 0).wait_send()

            @pl.when(z > s)
            def _():
                rs(s, c, 1).wait_send()

        for k in range(levels):
            tx(k, c).wait_send()
        return carry

    lax.fori_loop(0, ns, drain, 0)
    for d in range(1, n):
        ex(d).wait()
    total = ebuf[0]
    for s in range(1, n):
        total = total + ebuf[s]
    err_ref[0] = jnp.max(total) * (1.0 / (length * full))


def body(latents, noise, qkv_weight, qk_gains, out_weight, modulation, step_sizes, window_start):
    n = lax.axis_size("tensor")
    tm_size = lax.axis_size("tm")
    offset = window_start[0] + lax.axis_index("tm")
    _, length, width = latents.shape
    full = n * width
    mod_rows = lax.dynamic_index_in_dim(
        modulation.transpose(1, 0, 2), offset, 1, keepdims=False
    ).astype(f32)
    step_size = lax.dynamic_index_in_dim(step_sizes, offset, 0, keepdims=False)
    mod_rows = jnp.concatenate(
        [mod_rows, jnp.full((1, width), step_size), jnp.zeros((HDR - 4, width), f32)]
    )
    chunk = CHUNK
    nc = length // chunk
    ns = nc * SPLIT
    levels = tm_size.bit_length() - 1
    vmem = pl.BlockSpec(memory_space=pltpu.VMEM)
    hbm = pl.BlockSpec(memory_space=pl.ANY)
    dma = pltpu.SemaphoreType.DMA
    updated, velocity, err = pl.pallas_call(
        functools.partial(kernel, n, tm_size, chunk),
        out_shape=(
            jax.ShapeDtypeStruct((length, width), f32),
            jax.ShapeDtypeStruct((length, width), bf16),
            jax.ShapeDtypeStruct((1,), f32),
        ),
        in_specs=[vmem, hbm, hbm, vmem, hbm, vmem],
        out_specs=(vmem, vmem, pl.BlockSpec(memory_space=pltpu.SMEM)),
        scratch_shapes=[
            pltpu.VMEM((n, HDR + length, width), bf16),
            pltpu.VMEM((max(3 * full, (n + levels) * length), width), bf16),
            pltpu.VMEM((width, full), bf16),
            pltpu.VMEM((3, length, width), bf16),
            pltpu.VMEM((n + 1, length, width), bf16),
            pltpu.VMEM((levels, length, width), bf16),
            pltpu.VMEM((length, width), bf16),
            pltpu.VMEM((length, 3 * width), f32),
            pltpu.VMEM((chunk, width), bf16),
            pltpu.VMEM((8, width), f32),
            pltpu.VMEM((n, 8, 128), f32),
            pltpu.VMEM((n, 16, length), f32),
            pltpu.VMEM((16, length), f32),
            dma((5,)),
            dma((2, n, nc + 1)),
            dma((n, nc + 1)),
            dma((2, n, ns)),
            dma((2, n, ns)),
            dma((levels, ns)),
            dma((levels, ns)),
            dma((n,)),
            dma((n,)),
            dma((n,)),
            dma((n,)),
        ],
        compiler_params=pltpu.CompilerParams(
            collective_id=0, has_side_effects=True, vmem_limit_bytes=62 * 2**20
        ),
    )(
        latents[0], noise[0], qkv_weight.transpose(1, 0, 2), qk_gains, out_weight,
        mod_rows,
    )
    return (updated[None], velocity[None], err)


def solution(mesh):
    return jax.shard_map(
        body,
        mesh=mesh,
        in_specs=(
            P("tm", None, "tensor"),
            P("tm", None, "tensor"),
            P(None, None, "tensor"),
            P(None, "tensor"),
            P("tensor", None),
            P(None, None, "tensor"),
            P(),
            P(),
        ),
        out_specs=(P("tm", None, "tensor"), P("tm", None, "tensor"), P("tm")),
        check_vma=False,
    )
```

```python
import functools
import math

import jax
import jax.numpy as jnp
from jax import lax
from jax.experimental import pallas as pl
from jax.experimental.pallas import tpu as pltpu
from jax.sharding import PartitionSpec as P

HEAD = 128
HDR = 16
CHUNK = 256
SPLIT = 2
epsilon = 1e-06
f32 = jnp.float32
bf16 = jnp.bfloat16


def kernel(
    n, tm_size, chunk,
    x_ref, noise_hbm, w_hbm, gains_ref, wo_hbm, mod_ref,
    upd_ref, vel_ref, err_ref,
    gat, wbuf, wo, qkv, rbuf, trecv, noise, acc, att, erracc, ebuf, sums, stat,
    load_sem, ag_send, ag_recv, rs_send, rs_recv, t_send, t_recv, e_send, e_recv,
    s_send, s_recv,
):
    z = lax.axis_index("tensor")
    slot = lax.axis_index("tm")
    length, width = x_ref.shape
    full = n * width
    nc = length // chunk
    sub = chunk // SPLIT
    ns = nc * SPLIT
    heads = width // HEAD
    levels = tm_size.bit_length() - 1
    first = slot == 0

    loads = [
        pltpu.make_async_copy(
            w_hbm.at[j], wbuf.at[pl.ds(j * full, full)], load_sem.at[j]
        )
        for j in range(3)
    ]
    loads.append(pltpu.make_async_copy(wo_hbm, wo, load_sem.at[3]))
    loads.append(pltpu.make_async_copy(noise_hbm, noise, load_sem.at[4]))

    def crows(c, base=0):
        return pl.ds(pl.multiple_of(base + c * chunk, 16), chunk)

    def srows(c):
        return pl.ds(pl.multiple_of(c * sub, 16), sub)

    partners = []
    for k in range(levels):
        bit = lax.rem(slot // (1 << k), 2)
        partners.append((slot + (1 - 2 * bit) * (1 << k), bit))

    barrier = pltpu.get_barrier_semaphore()
    for d in range(1, n):
        pl.semaphore_signal(
            barrier, inc=1, device_id={"tensor": lax.rem(z + d, n)},
            device_id_type=pl.DeviceIdType.MESH,
        )
    for partner, _ in partners:
        pl.semaphore_signal(
            barrier, inc=1, device_id={"tm": partner},
            device_id_type=pl.DeviceIdType.MESH,
        )

    for load in loads:
        load.start()

    gat[z, pl.ds(0, HDR), :] = mod_ref[...].astype(bf16)

    def cast(c, carry):
        gat[z, crows(c, HDR), :] = x_ref[crows(c), :].astype(bf16)
        return carry

    lax.fori_loop(0, nc, cast, 0)
    pl.semaphore_wait(barrier, n - 1 + levels)

    right, left = lax.rem(z + 1, n), lax.rem(z + n - 1, n)
    half = n // 2

    def away(way, k):
        return lax.rem(z + k, n) if way == 0 else lax.rem(z + n - k, n)

    def reach(way, c, count):
        if c is None:
            return half - way
        early = c < count // 2
        return jnp.where(early, half - way, half - 1 + way)

    def ag(s, c, way):
        rows = pl.ds(0, HDR) if c is None else crows(c, HDR)
        i = nc if c is None else c
        return pltpu.make_async_remote_copy(
            src_ref=gat.at[s, rows], dst_ref=gat.at[s, rows],
            send_sem=ag_send.at[way, s, i], recv_sem=ag_recv.at[s, i],
            device_id={"tensor": right if way == 0 else left},
            device_id_type=pl.DeviceIdType.MESH,
        )

    def own(c):
        ag(z, c, 0).start()
        ag(z, c, 1).start()

    def forward(d, c):
        for way in (0, 1):
            s = away(1 - way, d)

            @pl.when(d <= reach(way, c, nc))
            def _(s=s, way=way):
                ag(s, c, way).wait_recv()

                @pl.when(d < reach(way, c, nc))
                def _():
                    ag(s, c, way).start()

    def own_all():
        own(None)

        def own_loop(c, carry):
            own(c)
            return carry

        lax.fori_loop(0, nc, own_loop, 0)

    own_all()

    ones = jnp.ones((8, width), bf16)

    def row_sum(rows):
        return lax.dot_general(
            ones, rows, (((1,), (1,)), ((), ())), preferred_element_type=f32
        )

    def count(c, carry):
        part = gat[z, crows(c, HDR), :]
        square = part.astype(f32) * part.astype(f32)
        high = square.astype(bf16)
        low = (square - high.astype(f32)).astype(bf16)
        lanes = pl.ds(pl.multiple_of(c * chunk, 128), chunk)
        sums[z, 0:8, lanes] = row_sum(part)
        sums[z, 8:16, lanes] = row_sum(high) + row_sum(low)
        return carry

    lax.fori_loop(0, nc, count, 0)

    def sx(d):
        return pltpu.make_async_remote_copy(
            src_ref=sums.at[z], dst_ref=sums.at[z],
            send_sem=s_send.at[d], recv_sem=s_recv.at[d],
            device_id={"tensor": lax.rem(z + d, n)}, device_id_type=pl.DeviceIdType.MESH,
        )

    for d in range(1, n):
        sx(d).start()

    def drain_gather():
        def one(c, carry):
            drain_one(c)
            return carry

        drain_one(None)
        lax.fori_loop(0, nc, one, 0)

    def drain_one(c):
        for way in (0, 1):
            for e in range(half):
                @pl.when(e < reach(way, c, nc))
                def _(way=way, e=e):
                    ag(away(1 - way, e), c, way).wait_send()

    for load in loads:
        load.wait()
    for d in range(1, n):
        sx(d).wait()

    total = sums[0]
    for s in range(1, n):
        total = total + sums[s]
    mean_row = total[0:8] * (1.0 / full)
    stat[0:8, :] = mean_row
    stat[8:16, :] = lax.rsqrt(total[8:16] * (1.0 / full) - mean_row * mean_row + epsilon)

    def accumulate(s, c, begin):
        lanes = pl.ds(pl.multiple_of(c * chunk, 128), chunk)
        columns = jnp.transpose(stat[:, lanes])
        head_rows = gat[s, pl.ds(0, HDR), :].astype(f32)
        part = gat[s, crows(c, HDR), :].astype(f32)
        rows = (
            (part - columns[:, 0:1]) * columns[:, 8:9] * (1.0 + head_rows[1:2]) + head_rows[0:1]
        ).astype(bf16)
        for j in range(3):
            cols = slice(j * width, (j + 1) * width)
            depth = pl.ds(pl.multiple_of(j * full + s * width, 128), width)
            out = jnp.dot(rows, wbuf[depth, :], preferred_element_type=f32)
            if begin:
                acc[crows(c), cols] = out
            else:
                acc[crows(c), cols] += out

    def own_part(c, carry):
        accumulate(z, c, True)
        return carry

    lax.fori_loop(0, nc, own_part, 0)

    def finish(c):
        for j in range(3):
            for h in range(heads):
                cols = slice(h * HEAD, (h + 1) * HEAD)
                vec = acc[crows(c), j * width + h * HEAD : j * width + (h + 1) * HEAD]
                if j < 2:
                    power = jnp.mean(vec * vec, axis=1, keepdims=True)
                    vec = vec * lax.rsqrt(power + epsilon) * gains_ref[j : j + 1, cols]
                qkv[j, crows(c), cols] = vec.astype(bf16)

    def distance(d, carry):
        forward(d, None)

        def one(c, carry):
            forward(d, c)

            for way in (0, 1):
                @pl.when(d <= reach(way, c, nc))
                def _(way=way):
                    accumulate(away(1 - way, d), c, False)

            @pl.when(d == half)
            def _():
                finish(c)

            return carry

        lax.fori_loop(0, nc, one, 0)
        return carry

    lax.fori_loop(1, half + 1, distance, 0)

    def prow(t, c):
        return pl.ds(pl.multiple_of(t * length + c * sub, 16), sub)

    def rs(t, c, way):
        if way == 0:
            place = t
        else:
            place = jnp.where(t == left, n, t)
        return pltpu.make_async_remote_copy(
            src_ref=wbuf.at[prow(t, c)], dst_ref=rbuf.at[place, srows(c)],
            send_sem=rs_send.at[way, t, c], recv_sem=rs_recv.at[way, t, c],
            device_id={"tensor": right if way == 0 else left},
            device_id_type=pl.DeviceIdType.MESH,
        )

    def tx(k, c):
        return pltpu.make_async_remote_copy(
            src_ref=wbuf.at[prow(n + k, c)], dst_ref=trecv.at[k, srows(c)],
            send_sem=t_send.at[k, c], recv_sem=t_recv.at[k, c],
            device_id={"tm": partners[k][0]}, device_id_type=pl.DeviceIdType.MESH,
        )

    exponent = math.log2(math.e) / math.sqrt(HEAD)

    def stage_attend(c):
        def one_head(h, carry):
            cols = pl.ds(pl.multiple_of(h * HEAD, HEAD), HEAD)
            scores = lax.dot_general(
                qkv[0, crows(c), cols], qkv[1, :, cols], (((1,), (1,)), ((), ())),
                preferred_element_type=f32,
            )
            top = jnp.max(scores, axis=1, keepdims=True)
            weights = jnp.exp2((scores - top) * exponent)
            norm = jnp.sum(weights, axis=1, keepdims=True)
            out = jnp.dot(weights.astype(bf16), qkv[2, :, cols], preferred_element_type=f32)
            att[:, cols] = (out / norm).astype(bf16)
            return carry

        lax.fori_loop(0, heads, one_head, 0, unroll=3)

        def one_part(t, carry):
            cols = pl.ds(pl.multiple_of(t * width, 128), width)
            part = jnp.dot(att[...], wo[:, cols], preferred_element_type=f32)
            wbuf[pl.ds(pl.multiple_of(t * length + c * chunk, 16), chunk), :] = part.astype(
                bf16
            )
            return carry

        lax.fori_loop(0, n, one_part, 0)

        for p in range(SPLIT):
            sc = c * SPLIT + p
            for way in (0, 1):
                rs(away(way, reach(way, sc, ns)), sc, way).start()

    def stage_join(c):
        for k in range(half - 1, 0, -1):
            for way in (0, 1):
                t = away(way, k)

                @pl.when(k < reach(way, c, ns))
                def _(t=t, way=way):
                    rs(t, c, way).wait_recv()
                    wbuf[prow(t, c), :] = (
                        wbuf[prow(t, c), :].astype(f32) + rbuf[t, srows(c), :].astype(f32)
                    ).astype(bf16)
                    rs(t, c, way).start()

    def stage_velocity(c):
        rows = srows(c)

        rs(z, c, 0).wait_recv()
        pltpu.make_async_remote_copy(
            src_ref=wbuf.at[prow(z, c)], dst_ref=rbuf.at[n, rows],
            send_sem=rs_send.at[1, z, c], recv_sem=rs_recv.at[1, z, c],
            device_id={"tensor": left}, device_id_type=pl.DeviceIdType.MESH,
        ).wait_recv()
        branch = (
            wbuf[prow(z, c), :].astype(f32)
            + rbuf[z, rows, :].astype(f32)
            + rbuf[n, rows, :].astype(f32)
        )
        state = x_ref[rows, :]
        velocity = state + mod_ref[2:3, :] * branch
        vel_ref[rows, :] = velocity.astype(bf16)
        start = jnp.where(first, state, jnp.zeros_like(state))
        upd_ref[rows, :] = start
        wbuf[prow(n, c), :] = (
            noise[rows, :].astype(f32) - mod_ref[3:4, :] * velocity + start
        ).astype(bf16)
        tx(0, c).start()

    def stage_prefix(k, c):
        rows = srows(c)
        tx(k, c).wait_recv()
        arrived = trecv[k, rows, :].astype(f32)
        if k < levels - 1:
            wbuf[prow(n + k + 1, c), :] = (
                wbuf[prow(n + k, c), :].astype(f32) + arrived
            ).astype(bf16)
            tx(k + 1, c).start()
        keep = partners[k][1].astype(f32)
        now = upd_ref[rows, :] + keep * arrived
        upd_ref[rows, :] = now
        if k == levels - 1:
            change = now - x_ref[rows, :]
            erracc[...] += jnp.sum(
                (change * change).reshape(sub // 8, 8, width), axis=0
            )

    erracc[...] = jnp.zeros_like(erracc)
    lag = 5

    def turn(i, carry):
        @pl.when((i < ns) & (lax.rem(i, SPLIT) == 0))
        def _():
            stage_attend(i // SPLIT)

        @pl.when((i >= 1) & (i < ns + 1))
        def _():
            stage_join(i - 1)

        @pl.when((i >= lag) & (i < ns + lag))
        def _():
            stage_velocity(i - lag)

        for k in range(levels):
            @pl.when((i >= lag + 1 + k) & (i < ns + lag + 1 + k))
            def _(k=k):
                stage_prefix(k, i - (lag + 1 + k))

        return carry

    lax.fori_loop(0, ns + lag + levels, turn, 0)

    ebuf[z] = jnp.zeros((8, 128), f32) + jnp.sum(erracc[...])

    def ex(d):
        return pltpu.make_async_remote_copy(
            src_ref=ebuf.at[z], dst_ref=ebuf.at[z],
            send_sem=e_send.at[d], recv_sem=e_recv.at[d],
            device_id={"tensor": lax.rem(z + d, n)}, device_id_type=pl.DeviceIdType.MESH,
        )

    for d in range(1, n):
        ex(d).start()

    drain_gather()

    def drain(c, carry):
        for way in (0, 1):
            for k in range(1, half + 1):
                @pl.when(k <= reach(way, c, ns))
                def _(way=way, k=k):
                    rs(away(way, k), c, way).wait_send()

        for k in range(levels):
            tx(k, c).wait_send()
        return carry

    lax.fori_loop(0, ns, drain, 0)
    for d in range(1, n):
        ex(d).wait()
    total = ebuf[0]
    for s in range(1, n):
        total = total + ebuf[s]
    err_ref[0] = jnp.max(total) * (1.0 / (length * full))


def body(latents, noise, qkv_weight, qk_gains, out_weight, modulation, step_sizes, window_start):
    n = lax.axis_size("tensor")
    tm_size = lax.axis_size("tm")
    offset = window_start[0] + lax.axis_index("tm")
    _, length, width = latents.shape
    full = n * width
    mod_rows = lax.dynamic_index_in_dim(
        modulation.transpose(1, 0, 2), offset, 1, keepdims=False
    ).astype(f32)
    step_size = lax.dynamic_index_in_dim(step_sizes, offset, 0, keepdims=False)
    mod_rows = jnp.concatenate(
        [mod_rows, jnp.full((1, width), step_size), jnp.zeros((HDR - 4, width), f32)]
    )
    chunk = CHUNK
    nc = length // chunk
    ns = nc * SPLIT
    levels = tm_size.bit_length() - 1
    vmem = pl.BlockSpec(memory_space=pltpu.VMEM)
    hbm = pl.BlockSpec(memory_space=pl.ANY)
    dma = pltpu.SemaphoreType.DMA
    updated, velocity, err = pl.pallas_call(
        functools.partial(kernel, n, tm_size, chunk),
        out_shape=(
            jax.ShapeDtypeStruct((length, width), f32),
            jax.ShapeDtypeStruct((length, width), bf16),
            jax.ShapeDtypeStruct((1,), f32),
        ),
        in_specs=[vmem, hbm, hbm, vmem, hbm, vmem],
        out_specs=(vmem, vmem, pl.BlockSpec(memory_space=pltpu.SMEM)),
        scratch_shapes=[
            pltpu.VMEM((n, HDR + length, width), bf16),
            pltpu.VMEM((max(3 * full, (n + levels) * length), width), bf16),
            pltpu.VMEM((width, full), bf16),
            pltpu.VMEM((3, length, width), bf16),
            pltpu.VMEM((n + 1, length, width), bf16),
            pltpu.VMEM((levels, length, width), bf16),
            pltpu.VMEM((length, width), bf16),
            pltpu.VMEM((length, 3 * width), f32),
            pltpu.VMEM((chunk, width), bf16),
            pltpu.VMEM((8, width), f32),
            pltpu.VMEM((n, 8, 128), f32),
            pltpu.VMEM((n, 16, length), f32),
            pltpu.VMEM((16, length), f32),
            dma((5,)),
            dma((2, n, nc + 1)),
            dma((n, nc + 1)),
            dma((2, n, ns)),
            dma((2, n, ns)),
            dma((levels, ns)),
            dma((levels, ns)),
            dma((n,)),
            dma((n,)),
            dma((n,)),
            dma((n,)),
        ],
        compiler_params=pltpu.CompilerParams(
            collective_id=0, has_side_effects=True, vmem_limit_bytes=62 * 2**20
        ),
    )(
        latents[0], noise[0], qkv_weight.transpose(1, 0, 2), qk_gains, out_weight,
        mod_rows,
    )
    return (updated[None], velocity[None], err)


def solution(mesh):
    return jax.shard_map(
        body,
        mesh=mesh,
        in_specs=(
            P("tm", None, "tensor"),
            P("tm", None, "tensor"),
            P(None, None, "tensor"),
            P(None, "tensor"),
            P("tensor", None),
            P(None, None, "tensor"),
            P(),
            P(),
        ),
        out_specs=(P("tm", None, "tensor"), P("tm", None, "tensor"), P("tm")),
        check_vma=False,
    )
```

```python
import functools
import math

import jax
import jax.numpy as jnp
from jax import lax
from jax.experimental import pallas as pl
from jax.experimental.pallas import tpu as pltpu
from jax.sharding import PartitionSpec as P

HEAD = 128
HDR = 16
CHUNK = 256
SPLIT = 2
epsilon = 1e-06
f32 = jnp.float32
bf16 = jnp.bfloat16


def kernel(
    n, tm_size, chunk,
    x_ref, noise_hbm, w_hbm, gains_ref, wo_hbm, mod_ref,
    upd_ref, vel_ref, err_ref,
    gat, wbuf, wo, qs, kt, vs, rbuf, trecv, noise, acc, att, erracc, ebuf, sums, stat,
    load_sem, ag_send, ag_recv, rs_send, rs_recv, t_send, t_recv, e_send, e_recv,
    s_send, s_recv,
):
    z = lax.axis_index("tensor")
    slot = lax.axis_index("tm")
    length, width = x_ref.shape
    full = n * width
    nc = length // chunk
    sub = chunk // SPLIT
    ns = nc * SPLIT
    heads = width // HEAD
    levels = tm_size.bit_length() - 1
    first = slot == 0

    loads = [
        pltpu.make_async_copy(
            w_hbm.at[j], wbuf.at[pl.ds(j * full, full)], load_sem.at[j]
        )
        for j in range(3)
    ]
    loads.append(pltpu.make_async_copy(wo_hbm, wo, load_sem.at[3]))
    loads.append(pltpu.make_async_copy(noise_hbm, noise, load_sem.at[4]))

    def crows(c, base=0):
        return pl.ds(pl.multiple_of(base + c * chunk, 16), chunk)

    def srows(c):
        return pl.ds(pl.multiple_of(c * sub, 16), sub)

    partners = []
    for k in range(levels):
        bit = lax.rem(slot // (1 << k), 2)
        partners.append((slot + (1 - 2 * bit) * (1 << k), bit))

    barrier = pltpu.get_barrier_semaphore()
    for d in range(1, n):
        pl.semaphore_signal(
            barrier, inc=1, device_id={"tensor": lax.rem(z + d, n)},
            device_id_type=pl.DeviceIdType.MESH,
        )
    for partner, _ in partners:
        pl.semaphore_signal(
            barrier, inc=1, device_id={"tm": partner},
            device_id_type=pl.DeviceIdType.MESH,
        )

    for load in loads:
        load.start()

    gat[z, pl.ds(0, HDR), :] = mod_ref[...].astype(bf16)

    def cast(c, carry):
        gat[z, crows(c, HDR), :] = x_ref[crows(c), :].astype(bf16)
        return carry

    lax.fori_loop(0, nc, cast, 0)
    pl.semaphore_wait(barrier, n - 1 + levels)

    right, left = lax.rem(z + 1, n), lax.rem(z + n - 1, n)
    half = n // 2

    def away(way, k):
        return lax.rem(z + k, n) if way == 0 else lax.rem(z + n - k, n)

    def reach(way, c, count):
        if c is None:
            return half - way
        early = c < count // 2
        return jnp.where(early, half - way, half - 1 + way)

    def ag(s, c, way):
        rows = pl.ds(0, HDR) if c is None else crows(c, HDR)
        i = nc if c is None else c
        return pltpu.make_async_remote_copy(
            src_ref=gat.at[s, rows], dst_ref=gat.at[s, rows],
            send_sem=ag_send.at[way, s, i], recv_sem=ag_recv.at[s, i],
            device_id={"tensor": right if way == 0 else left},
            device_id_type=pl.DeviceIdType.MESH,
        )

    def own(c):
        ag(z, c, 0).start()
        ag(z, c, 1).start()

    def forward(d, c):
        for way in (0, 1):
            s = away(1 - way, d)

            @pl.when(d <= reach(way, c, nc))
            def _(s=s, way=way):
                ag(s, c, way).wait_recv()

                @pl.when(d < reach(way, c, nc))
                def _():
                    ag(s, c, way).start()

    def own_all():
        own(None)

        def own_loop(c, carry):
            own(c)
            return carry

        lax.fori_loop(0, nc, own_loop, 0)

    own_all()

    ones = jnp.ones((8, width), bf16)

    def row_sum(rows):
        return lax.dot_general(
            ones, rows, (((1,), (1,)), ((), ())), preferred_element_type=f32
        )

    def count(c, carry):
        part = gat[z, crows(c, HDR), :]
        square = part.astype(f32) * part.astype(f32)
        high = square.astype(bf16)
        low = (square - high.astype(f32)).astype(bf16)
        lanes = pl.ds(pl.multiple_of(c * chunk, 128), chunk)
        sums[z, 0:8, lanes] = row_sum(part)
        sums[z, 8:16, lanes] = row_sum(high) + row_sum(low)
        return carry

    lax.fori_loop(0, nc, count, 0)

    def sx(d):
        return pltpu.make_async_remote_copy(
            src_ref=sums.at[z], dst_ref=sums.at[z],
            send_sem=s_send.at[d], recv_sem=s_recv.at[d],
            device_id={"tensor": lax.rem(z + d, n)}, device_id_type=pl.DeviceIdType.MESH,
        )

    for d in range(1, n):
        sx(d).start()

    def drain_gather():
        def one(c, carry):
            drain_one(c)
            return carry

        drain_one(None)
        lax.fori_loop(0, nc, one, 0)

    def drain_one(c):
        for way in (0, 1):
            for e in range(half):
                @pl.when(e < reach(way, c, nc))
                def _(way=way, e=e):
                    ag(away(1 - way, e), c, way).wait_send()

    for load in loads:
        load.wait()
    for d in range(1, n):
        sx(d).wait()

    total = sums[0]
    for s in range(1, n):
        total = total + sums[s]
    mean_row = total[0:8] * (1.0 / full)
    stat[0:8, :] = mean_row
    stat[8:16, :] = lax.rsqrt(total[8:16] * (1.0 / full) - mean_row * mean_row + epsilon)

    def accumulate(s, c, begin):
        lanes = pl.ds(pl.multiple_of(c * chunk, 128), chunk)
        columns = jnp.transpose(stat[:, lanes])
        head_rows = gat[s, pl.ds(0, HDR), :].astype(f32)
        part = gat[s, crows(c, HDR), :].astype(f32)
        rows = (
            (part - columns[:, 0:1]) * columns[:, 8:9] * (1.0 + head_rows[1:2]) + head_rows[0:1]
        ).astype(bf16)
        for j in range(3):
            cols = slice(j * width, (j + 1) * width)
            depth = pl.ds(pl.multiple_of(j * full + s * width, 128), width)
            out = jnp.dot(rows, wbuf[depth, :], preferred_element_type=f32)
            if begin:
                acc[crows(c), cols] = out
            else:
                acc[crows(c), cols] += out

    def own_part(c, carry):
        accumulate(z, c, True)
        return carry

    lax.fori_loop(0, nc, own_part, 0)

    def finish(c):
        for j in range(3):
            for h in range(heads):
                cols = slice(h * HEAD, (h + 1) * HEAD)
                vec = acc[crows(c), j * width + h * HEAD : j * width + (h + 1) * HEAD]
                if j < 2:
                    power = jnp.mean(vec * vec, axis=1, keepdims=True)
                    vec = vec * lax.rsqrt(power + epsilon) * gains_ref[j : j + 1, cols]
                if j == 0:
                    qs[crows(c), cols] = vec.astype(bf16)
                elif j == 1:
                    lanes = pl.ds(pl.multiple_of(c * chunk, 128), chunk)
                    kt[cols, lanes] = jnp.transpose(vec).astype(bf16)
                else:
                    vs[crows(c), 2 * h * HEAD : (2 * h + 1) * HEAD] = vec.astype(bf16)
                    vs[crows(c), (2 * h + 1) * HEAD : (2 * h + 2) * HEAD] = jnp.ones(
                        (chunk, HEAD), bf16
                    )

    def distance(d, carry):
        forward(d, None)

        def one(c, carry):
            forward(d, c)

            for way in (0, 1):
                @pl.when(d <= reach(way, c, nc))
                def _(way=way):
                    accumulate(away(1 - way, d), c, False)

            @pl.when(d == half)
            def _():
                finish(c)

            return carry

        lax.fori_loop(0, nc, one, 0)
        return carry

    lax.fori_loop(1, half + 1, distance, 0)

    def prow(t, c):
        return pl.ds(pl.multiple_of(t * length + c * sub, 16), sub)

    def rs(t, c, way):
        if way == 0:
            place = t
        else:
            place = jnp.where(t == left, n, t)
        return pltpu.make_async_remote_copy(
            src_ref=wbuf.at[prow(t, c)], dst_ref=rbuf.at[place, srows(c)],
            send_sem=rs_send.at[way, t, c], recv_sem=rs_recv.at[way, t, c],
            device_id={"tensor": right if way == 0 else left},
            device_id_type=pl.DeviceIdType.MESH,
        )

    def tx(k, c):
        return pltpu.make_async_remote_copy(
            src_ref=wbuf.at[prow(n + k, c)], dst_ref=trecv.at[k, srows(c)],
            send_sem=t_send.at[k, c], recv_sem=t_recv.at[k, c],
            device_id={"tm": partners[k][0]}, device_id_type=pl.DeviceIdType.MESH,
        )

    exponent = math.log2(math.e) / math.sqrt(HEAD)

    def stage_attend(c):
        def one_head(h, carry):
            cols = pl.ds(pl.multiple_of(h * HEAD, HEAD), HEAD)
            wide = pl.ds(pl.multiple_of(h * 2 * HEAD, 2 * HEAD), 2 * HEAD)
            scores = jnp.dot(qs[crows(c), cols], kt[cols, :], preferred_element_type=f32)
            top = jnp.max(scores, axis=1, keepdims=True)
            weights = jnp.exp2((scores - top) * exponent).astype(bf16)
            out = jnp.dot(weights, vs[:, wide], preferred_element_type=f32)
            att[:, cols] = (out[:, :HEAD] / out[:, HEAD:]).astype(bf16)
            return carry

        lax.fori_loop(0, heads, one_head, 0, unroll=3)

        def one_part(t, carry):
            cols = pl.ds(pl.multiple_of(t * width, 128), width)
            part = jnp.dot(att[...], wo[:, cols], preferred_element_type=f32)
            wbuf[pl.ds(pl.multiple_of(t * length + c * chunk, 16), chunk), :] = part.astype(
                bf16
            )
            return carry

        lax.fori_loop(0, n, one_part, 0)

        for p in range(SPLIT):
            sc = c * SPLIT + p
            for way in (0, 1):
                rs(away(way, reach(way, sc, ns)), sc, way).start()

    def stage_join(c):
        for k in range(half - 1, 0, -1):
            for way in (0, 1):
                t = away(way, k)

                @pl.when(k < reach(way, c, ns))
                def _(t=t, way=way):
                    rs(t, c, way).wait_recv()
                    wbuf[prow(t, c), :] = (
                        wbuf[prow(t, c), :].astype(f32) + rbuf[t, srows(c), :].astype(f32)
                    ).astype(bf16)
                    rs(t, c, way).start()

    def stage_velocity(c):
        rows = srows(c)

        rs(z, c, 0).wait_recv()
        pltpu.make_async_remote_copy(
            src_ref=wbuf.at[prow(z, c)], dst_ref=rbuf.at[n, rows],
            send_sem=rs_send.at[1, z, c], recv_sem=rs_recv.at[1, z, c],
            device_id={"tensor": left}, device_id_type=pl.DeviceIdType.MESH,
        ).wait_recv()
        branch = (
            wbuf[prow(z, c), :].astype(f32)
            + rbuf[z, rows, :].astype(f32)
            + rbuf[n, rows, :].astype(f32)
        )
        state = x_ref[rows, :]
        velocity = state + mod_ref[2:3, :] * branch
        vel_ref[rows, :] = velocity.astype(bf16)
        start = jnp.where(first, state, jnp.zeros_like(state))
        upd_ref[rows, :] = start
        wbuf[prow(n, c), :] = (
            noise[rows, :].astype(f32) - mod_ref[3:4, :] * velocity + start
        ).astype(bf16)
        tx(0, c).start()

    def stage_prefix(k, c):
        rows = srows(c)
        tx(k, c).wait_recv()
        arrived = trecv[k, rows, :].astype(f32)
        if k < levels - 1:
            wbuf[prow(n + k + 1, c), :] = (
                wbuf[prow(n + k, c), :].astype(f32) + arrived
            ).astype(bf16)
            tx(k + 1, c).start()
        keep = partners[k][1].astype(f32)
        now = upd_ref[rows, :] + keep * arrived
        upd_ref[rows, :] = now
        if k == levels - 1:
            change = now - x_ref[rows, :]
            erracc[...] += jnp.sum(
                (change * change).reshape(sub // 8, 8, width), axis=0
            )

    erracc[...] = jnp.zeros_like(erracc)
    lag = 3

    def turn(i, carry):
        @pl.when((i < ns) & (lax.rem(i, SPLIT) == 0))
        def _():
            stage_attend(i // SPLIT)

        @pl.when((i >= 1) & (i < ns + 1))
        def _():
            stage_join(i - 1)

        @pl.when((i >= lag) & (i < ns + lag))
        def _():
            stage_velocity(i - lag)

        for k in range(levels):
            @pl.when((i >= lag + 1 + k) & (i < ns + lag + 1 + k))
            def _(k=k):
                stage_prefix(k, i - (lag + 1 + k))

        return carry

    lax.fori_loop(0, ns + lag + levels, turn, 0)

    ebuf[z] = jnp.zeros((8, 128), f32) + jnp.sum(erracc[...])

    def ex(d):
        return pltpu.make_async_remote_copy(
            src_ref=ebuf.at[z], dst_ref=ebuf.at[z],
            send_sem=e_send.at[d], recv_sem=e_recv.at[d],
            device_id={"tensor": lax.rem(z + d, n)}, device_id_type=pl.DeviceIdType.MESH,
        )

    for d in range(1, n):
        ex(d).start()

    drain_gather()

    def drain(c, carry):
        for way in (0, 1):
            for k in range(1, half + 1):
                @pl.when(k <= reach(way, c, ns))
                def _(way=way, k=k):
                    rs(away(way, k), c, way).wait_send()

        for k in range(levels):
            tx(k, c).wait_send()
        return carry

    lax.fori_loop(0, ns, drain, 0)
    for d in range(1, n):
        ex(d).wait()
    total = ebuf[0]
    for s in range(1, n):
        total = total + ebuf[s]
    err_ref[0] = jnp.max(total) * (1.0 / (length * full))


def body(latents, noise, qkv_weight, qk_gains, out_weight, modulation, step_sizes, window_start):
    n = lax.axis_size("tensor")
    tm_size = lax.axis_size("tm")
    offset = window_start[0] + lax.axis_index("tm")
    _, length, width = latents.shape
    full = n * width
    mod_rows = lax.dynamic_index_in_dim(
        modulation.transpose(1, 0, 2), offset, 1, keepdims=False
    ).astype(f32)
    step_size = lax.dynamic_index_in_dim(step_sizes, offset, 0, keepdims=False)
    mod_rows = jnp.concatenate(
        [mod_rows, jnp.full((1, width), step_size), jnp.zeros((HDR - 4, width), f32)]
    )
    chunk = CHUNK
    nc = length // chunk
    ns = nc * SPLIT
    levels = tm_size.bit_length() - 1
    vmem = pl.BlockSpec(memory_space=pltpu.VMEM)
    hbm = pl.BlockSpec(memory_space=pl.ANY)
    dma = pltpu.SemaphoreType.DMA
    updated, velocity, err = pl.pallas_call(
        functools.partial(kernel, n, tm_size, chunk),
        out_shape=(
            jax.ShapeDtypeStruct((length, width), f32),
            jax.ShapeDtypeStruct((length, width), bf16),
            jax.ShapeDtypeStruct((1,), f32),
        ),
        in_specs=[vmem, hbm, hbm, vmem, hbm, vmem],
        out_specs=(vmem, vmem, pl.BlockSpec(memory_space=pltpu.SMEM)),
        scratch_shapes=[
            pltpu.VMEM((n, HDR + length, width), bf16),
            pltpu.VMEM((max(3 * full, (n + levels) * length), width), bf16),
            pltpu.VMEM((width, full), bf16),
            pltpu.VMEM((length, width), bf16),
            pltpu.VMEM((width, length), bf16),
            pltpu.VMEM((length, 2 * width), bf16),
            pltpu.VMEM((n + 1, length, width), bf16),
            pltpu.VMEM((levels, length, width), bf16),
            pltpu.VMEM((length, width), bf16),
            pltpu.VMEM((length, 3 * width), f32),
            pltpu.VMEM((chunk, width), bf16),
            pltpu.VMEM((8, width), f32),
            pltpu.VMEM((n, 8, 128), f32),
            pltpu.VMEM((n, 16, length), f32),
            pltpu.VMEM((16, length), f32),
            dma((5,)),
            dma((2, n, nc + 1)),
            dma((n, nc + 1)),
            dma((2, n, ns)),
            dma((2, n, ns)),
            dma((levels, ns)),
            dma((levels, ns)),
            dma((n,)),
            dma((n,)),
            dma((n,)),
            dma((n,)),
        ],
        compiler_params=pltpu.CompilerParams(
            collective_id=0, has_side_effects=True, vmem_limit_bytes=62 * 2**20
        ),
    )(
        latents[0], noise[0], qkv_weight.transpose(1, 0, 2), qk_gains, out_weight,
        mod_rows,
    )
    return (updated[None], velocity[None], err)


def solution(mesh):
    return jax.shard_map(
        body,
        mesh=mesh,
        in_specs=(
            P("tm", None, "tensor"),
            P("tm", None, "tensor"),
            P(None, None, "tensor"),
            P(None, "tensor"),
            P("tensor", None),
            P(None, None, "tensor"),
            P(),
            P(),
        ),
        out_specs=(P("tm", None, "tensor"), P("tm", None, "tensor"), P("tm")),
        check_vma=False,
    )
```
